32 devices in a mesh: pipe: 2 (over x), tensor: 4 (over y, core), dp: 4 (over z).
Axes of the slice: x: 2, y: 2, z: 4, core: 2. Of those that a mesh axis runs over, the one named last changes fastest.
Arguments:
- fwd_qkv: bfloat16 [3, 8, 256, 8192], P(None, ('pipe', 'dp'), None, 'tensor'), may hold values from -8 to 8, as said below
- fwd_segments: int32 [8, 256], P(('pipe', 'dp')), may hold values from 0 to 15, as said below
- parked: bfloat16 [3, 8, 256, 8192], P(None, ('pipe', 'dp'), 'tensor'), may hold values from -8 to 8, as said below
- bwd_segments: int32 [8, 256], P(('pipe', 'dp')), may hold values from 0 to 15, as said below
- grad_out: bfloat16 [8, 256, 8192], P(('pipe', 'dp'), None, 'tensor'), may hold values from -6 to 6
- loss_tokens: int32 [8], P(('pipe', 'dp')), may hold values from 1 to 256
Outputs:
- received: bfloat16 [8, 256, 8192], P(('pipe', 'dp'), None, 'tensor')
- grads: bfloat16 [3, 8, 256, 8192], P(None, ('pipe', 'dp'), None, 'tensor')
The draws below stay inside these ranges and needn't reach their ends.
Inputs may be any that keep to these rules, and one draw needn't show every extreme that they name: `fwd_qkv`: Real-valued. `parked`: Real-valued. `fwd_segments`: in each slot the numbers start at 0, never fall, and change only at positions that are multiples of 16. `bwd_segments`: in each slot the numbers start at 0, never fall, and change only at positions that are multiples of 16.
All inputs are finite; a program needn't handle non-finite values.
Results may differ from the reference program's by a relative error of at most 0.0051.
Values may be sent and summed in bfloat16 or wider, within the bound.
A program may use at most 128 MiB of HBM per device.

```python
import jax
import jax.numpy as jnp
from jax import lax

HEAD_DIM = 128
SEQ = 256
FEAT = 8192
MICRO = 8
N_PIPE = 2
N_DP = 4


def stacked_draw(key):
    key_main = jax.random.fold_in(key, 0)
    values = jnp.clip(jax.random.normal(key_main, (3, MICRO, SEQ, FEAT), jnp.float32), -4.0, 4.0)
    return values.astype(jnp.bfloat16)


def segment_draw(key):
    key_rate, key_cut = jax.random.split(key, 2)
    cell_count = SEQ // 16
    rate = jax.random.randint(key_rate, (MICRO, 1), 1, 8)
    rate = jnp.where(jnp.arange(MICRO)[:, None] == 0, 8, rate)
    cuts = jax.random.randint(key_cut, (MICRO, cell_count), 0, 8) < rate
    cuts = jnp.where(jnp.arange(cell_count)[None, :] == 0, False, cuts)
    numbers = jnp.cumsum(cuts.astype(jnp.int32), axis=1)
    return jnp.repeat(numbers, 16, axis=1).astype(jnp.int32)


def draw_fwd_qkv(key, part):
    key = jax.random.fold_in(key, 11)
    return stacked_draw(key)


def draw_parked(key, part):
    key = jax.random.fold_in(key, 13)
    return stacked_draw(key)


def draw_fwd_segments(key, part):
    key = jax.random.fold_in(key, 17)
    return segment_draw(key)


def draw_bwd_segments(key, part):
    key = jax.random.fold_in(key, 19)
    return segment_draw(key)


def draw_loss_tokens(key, part):
    key = jax.random.fold_in(key, 23)
    replica = jnp.arange(MICRO) % N_DP
    spread = jax.random.randint(key, (MICRO,), 0, SEQ // (2 * N_DP))
    counts = jnp.where(replica == N_DP - 1, SEQ, (replica + 1) * (SEQ // N_DP) - spread)
    return counts.astype(jnp.int32)


def block_levels(rng, shape, shards, smallest, largest):
    level = 1.0
    for dim, parts in shards:
        steps = jax.random.uniform(jax.random.fold_in(jax.random.fold_in(rng, 6), dim), (parts,), jnp.float32, smallest / len(shards), largest / len(shards))
        level = level * jnp.repeat(jnp.exp(steps), shape[dim] // parts).reshape((-1,) + (1,) * (len(shape) - 1 - dim))
    return level


def scatter_about(own_key, shape, scale, limit, shards=(), kind=jnp.bfloat16):
    entries = jax.random.normal(own_key, shape, jnp.float32) * scale
    if len(shards) > 0:
        entries = block_levels(own_key, shape, shards, -0.22, 0.18) * entries
    return jnp.clip(entries, min=-limit, max=limit).astype(kind)


def setup_inputs(seed: int = 0) -> dict:
    seeds = jax.random.split(jax.random.key(seed), 7)
    return {
        "fwd_qkv": draw_fwd_qkv(jax.random.fold_in(seeds[6], 71), 0),
        "fwd_segments": draw_fwd_segments(jax.random.fold_in(seeds[6], 71), 0),
        "parked": draw_parked(jax.random.fold_in(seeds[6], 71), 0),
        "bwd_segments": draw_bwd_segments(jax.random.fold_in(seeds[6], 71), 0),
        "grad_out": scatter_about(seeds[4], (MICRO, SEQ, FEAT), 1.0, 6.0, ((0, 8), (2, 4))),
        "loss_tokens": draw_loss_tokens(jax.random.fold_in(seeds[6], 71), 0),
    }


def probabilities(queries, key_rows, segment):
    length = queries.shape[0]
    head_count = queries.shape[1] // HEAD_DIM
    query_heads = queries.reshape(length, head_count, HEAD_DIM).astype(jnp.float32)
    key_heads = key_rows.reshape(length, head_count, HEAD_DIM).astype(jnp.float32)
    logits = jnp.einsum("qhd,khd->hqk", query_heads, key_heads) * (HEAD_DIM ** -0.5)
    inside = segment[:, None] == segment[None, :]
    logits = jnp.where(inside[None], logits, jnp.float32(-1e30))
    highest = jnp.max(logits, axis=-1, keepdims=True)
    weights = jnp.exp(logits - highest)
    return weights / jnp.sum(weights, axis=-1, keepdims=True)


def rounded(values):
    return lax.optimization_barrier(values.astype(jnp.bfloat16)).astype(jnp.float32)


def attend(queries, key_rows, value_rows, segment):
    length = queries.shape[0]
    head_count = queries.shape[1] // HEAD_DIM
    probs_low = rounded(probabilities(queries, key_rows, segment))
    value_heads = value_rows.reshape(length, head_count, HEAD_DIM).astype(jnp.float32)
    mixed = jnp.einsum("hqk,khd->qhd", probs_low, value_heads)
    return mixed.reshape(length, head_count * HEAD_DIM).astype(jnp.bfloat16)


def attend_backward(queries, key_rows, value_rows, segment, upstream, factor):
    length = queries.shape[0]
    head_count = queries.shape[1] // HEAD_DIM
    probs = probabilities(queries, key_rows, segment)
    probs_low = rounded(probs)
    query_heads = queries.reshape(length, head_count, HEAD_DIM).astype(jnp.float32)
    key_heads = key_rows.reshape(length, head_count, HEAD_DIM).astype(jnp.float32)
    value_heads = value_rows.reshape(length, head_count, HEAD_DIM).astype(jnp.float32)
    upstream_heads = upstream.reshape(length, head_count, HEAD_DIM).astype(jnp.float32)
    grad_value = jnp.einsum("hqk,qhd->khd", probs_low, upstream_heads)
    grad_probs = jnp.einsum("qhd,khd->hqk", upstream_heads, value_heads)
    center = jnp.sum(probs * grad_probs, axis=-1, keepdims=True)
    grad_logits = rounded(probs * (grad_probs - center) * (HEAD_DIM ** -0.5))
    grad_query = jnp.einsum("hqk,khd->qhd", grad_logits, key_heads)
    grad_key = jnp.einsum("hqk,qhd->khd", grad_logits, query_heads)
    stacked = jnp.stack([grad_query, grad_key, grad_value]) * factor
    return stacked.reshape(3, length, head_count * HEAD_DIM).astype(jnp.bfloat16)


def reference(fwd_qkv, fwd_segments, parked, bwd_segments, grad_out, loss_tokens):
    forward_out = lax.map(lambda item: attend(item[0], item[1], item[2], item[3]),
                          (fwd_qkv[0], fwd_qkv[1], fwd_qkv[2], fwd_segments))
    received = jnp.roll(forward_out.reshape(N_PIPE, N_DP, SEQ, FEAT), 1, axis=0).reshape(MICRO, SEQ, FEAT)
    stash = jnp.flip(parked.reshape(3, N_PIPE, N_DP, SEQ, FEAT), axis=1).reshape(3, MICRO, SEQ, FEAT)
    upstream = jnp.roll(grad_out.reshape(N_PIPE, N_DP, SEQ, FEAT), -1, axis=0).reshape(MICRO, SEQ, FEAT)
    token_total = jnp.sum(loss_tokens.reshape(N_PIPE, N_DP).astype(jnp.float32), axis=1)
    factor = jnp.repeat(jnp.float32(N_DP * SEQ) / token_total, N_DP)
    grads = lax.map(lambda item: attend_backward(item[0], item[1], item[2], item[3], item[4], item[5]),
                    (stash[0], stash[1], stash[2], bwd_segments, upstream, factor))
    return received, jnp.transpose(grads, (1, 0, 2, 3))
```

```python
import functools

import jax
import jax.numpy as jnp
from jax import lax
from jax.experimental import pallas as pl
from jax.experimental.pallas import tpu as pltpu
from jax.sharding import PartitionSpec as P

HEAD_DIM = 128
SCALE = HEAD_DIM ** (-0.5)
GROUP = 2
MESH = pl.DeviceIdType.MESH


def dot(a, b, contract):
    return lax.dot_general(a, b, (contract, ((), ())), preferred_element_type=jnp.float32)


def softmax(query, key, bias):
    logits = dot(query, key, ((1,), (1,))) * SCALE + bias
    weights = jnp.exp(logits - jnp.max(logits, axis=-1, keepdims=True))
    return weights / jnp.sum(weights, axis=-1, keepdims=True)


def mask_bias(segment):
    length = segment.shape[1]
    along = jnp.broadcast_to(segment.astype(jnp.float32), (length, length))
    return jnp.where(along == along.T, jnp.float32(0), jnp.float32(-1e30))


def kernel(
    sections, tensors, replicas,
    fwd_hbm, fwd_seg_hbm, parked_hbm, bwd_seg_hbm, up_hbm, tokens_hbm,
    received_hbm, grads_hbm,
    fwd, out, stash, up, grads, fwd_bias, bwd_bias, fwd_seg, bwd_seg, tokens, token_tile, token_all,
    fwd_sem, up_sem, own_sem, small_sem,
    part_send, part_recv, out_send, out_recv, grad_send, grad_recv,
    seg_send, seg_recv, tok_send, tok_recv,
):
    section = lax.axis_index("pipe")
    lane = lax.axis_index("tensor")
    replica = lax.axis_index("dp")
    after = lax.rem(section + 1, sections)
    before = lax.rem(section + sections - 1, sections)
    mirror = sections - 1 - section
    length = fwd.shape[1]
    width = GROUP * HEAD_DIM
    columns = fwd.shape[2]
    groups = columns // width
    rows = parked_hbm.shape[2]

    barrier = pltpu.get_barrier_semaphore()
    greeted = 0
    for step in range(1, tensors):
        pl.semaphore_signal(barrier, inc=1, device_id={"tensor": lax.rem(lane + step, tensors)}, device_id_type=MESH)
        greeted += 1
    for other in range(replicas):
        pl.semaphore_signal(barrier, inc=1, device_id={"pipe": mirror, "dp": other}, device_id_type=MESH)
        greeted += 1
    if sections > 2:
        for other in (after, before):
            pl.semaphore_signal(barrier, inc=1, device_id={"pipe": other}, device_id_type=MESH)
            greeted += 1

    def span(g):
        return pl.ds(pl.multiple_of(g * width, width), width)

    def load_fwd(g):
        return pltpu.make_async_copy(fwd_hbm.at[:, 0, :, span(g)], fwd.at[:, :, span(g)], fwd_sem.at[g])

    def load_up(g):
        return pltpu.make_async_copy(up_hbm.at[0, :, span(g)], up.at[:, span(g)], up_sem.at[g])

    def my_rows(who):
        return pl.ds(pl.multiple_of(who * rows, rows), rows)

    def parked_span(who, g):
        return pl.ds(pl.multiple_of(who * columns + g * width, width), width)

    def load_own(g):
        return pltpu.make_async_copy(
            parked_hbm.at[:, 0, :, parked_span(lane, g)], stash.at[:, my_rows(lane), span(g)], own_sem.at[g]
        )

    def send_part(step, g):
        other = lax.rem(lane + step, tensors)
        return pltpu.make_async_remote_copy(
            src_ref=parked_hbm.at[:, 0, :, parked_span(other, g)],
            dst_ref=stash.at[:, my_rows(lane), span(g)],
            send_sem=part_send.at[step - 1, g],
            recv_sem=part_recv.at[step - 1, g],
            device_id={"tensor": other},
            device_id_type=MESH,
        )

    def recv_part(step, g):
        other = lax.rem(lane + tensors - step, tensors)
        return pltpu.make_async_remote_copy(
            src_ref=parked_hbm.at[:, 0, :, parked_span(lane, g)],
            dst_ref=stash.at[:, my_rows(other), span(g)],
            send_sem=part_send.at[step - 1, g],
            recv_sem=part_recv.at[step - 1, g],
            device_id={"tensor": other},
            device_id_type=MESH,
        )

    def send_out(g):
        return pltpu.make_async_remote_copy(
            src_ref=out.at[:, span(g)],
            dst_ref=received_hbm.at[0, :, span(g)],
            send_sem=out_send.at[g],
            recv_sem=out_recv.at[g],
            device_id={"pipe": after},
            device_id_type=MESH,
        )

    def send_grads(g):
        return pltpu.make_async_remote_copy(
            src_ref=grads.at[:, :, span(g)],
            dst_ref=grads_hbm.at[:, 0, :, span(g)],
            send_sem=grad_send.at[g],
            recv_sem=grad_recv.at[g],
            device_id={"pipe": mirror},
            device_id_type=MESH,
        )

    def send_tokens(other, mine):
        return pltpu.make_async_remote_copy(
            src_ref=token_tile,
            dst_ref=token_all.at[mine],
            send_sem=tok_send.at[other],
            recv_sem=tok_recv.at[mine],
            device_id={"pipe": mirror, "dp": other},
            device_id_type=MESH,
        )

    send_segment = pltpu.make_async_remote_copy(
        src_ref=bwd_seg_hbm,
        dst_ref=bwd_seg,
        send_sem=seg_send,
        recv_sem=seg_recv,
        device_id={"pipe": mirror},
        device_id_type=MESH,
    )

    seg_copy = pltpu.make_async_copy(fwd_seg_hbm, fwd_seg, small_sem.at[0])
    tok_copy = pltpu.make_async_copy(tokens_hbm, tokens, small_sem.at[1])
    seg_copy.start()
    tok_copy.start()
    pl.loop(0, groups)(lambda g: load_fwd(g).start())
    pl.loop(0, groups)(lambda g: load_own(g).start())
    pl.loop(0, groups)(lambda g: load_up(g).start())

    def forward(g):
        load_fwd(g).wait()
        for h in range(GROUP):
            cols = pl.ds(pl.multiple_of(g * width + h * HEAD_DIM, HEAD_DIM), HEAD_DIM)
            probs = softmax(fwd[0, :, cols], fwd[1, :, cols], fwd_bias[...])
            mixed = dot(probs.astype(jnp.bfloat16), fwd[2, :, cols], ((1,), (0,)))
            out[:, cols] = mixed.astype(jnp.bfloat16)

    tok_copy.wait()
    token_tile[...] = jnp.full(token_tile.shape, tokens[0], jnp.int32)

    pl.semaphore_wait(barrier, greeted)
    send_segment.start()
    for other in range(replicas):
        send_tokens(other, replica).start()

    @pl.loop(0, groups)
    def _(g):
        for step in range(1, tensors):
            send_part(step, g).start()

    seg_copy.wait()
    fwd_bias[...] = mask_bias(fwd_seg[...])

    @pl.loop(0, groups)
    def _(g):
        forward(g)
        send_out(g).start()

    send_segment.wait()
    bwd_bias[...] = mask_bias(bwd_seg[...])
    total = jnp.zeros((1, HEAD_DIM), jnp.float32)
    for other in range(replicas):
        send_tokens(other, other).wait_recv()
        total += token_all[other, 0:1, :].astype(jnp.float32)
    factor = jnp.float32(replicas * length) / total

    @pl.loop(0, groups)
    def _(g):
        load_own(g).wait()
        load_up(g).wait()
        for step in range(1, tensors):
            recv_part(step, g).wait_recv()
        for h in range(GROUP):
            cols = pl.ds(pl.multiple_of(g * width + h * HEAD_DIM, HEAD_DIM), HEAD_DIM)
            query, key, value, upstream = stash[0, :, cols], stash[1, :, cols], stash[2, :, cols], up[:, cols]
            probs = softmax(query, key, bwd_bias[...])
            grad_value = dot(probs.astype(jnp.bfloat16), upstream, ((0,), (0,)))
            grad_probs = dot(upstream, value, ((1,), (1,)))
            center = jnp.sum(probs * grad_probs, axis=-1, keepdims=True)
            grad_logits = (probs * (grad_probs - center) * SCALE).astype(jnp.bfloat16)
            grad_query = dot(grad_logits, key, ((1,), (0,)))
            grad_key = dot(grad_logits, query, ((0,), (0,)))
            grads[0, :, cols] = (grad_query * factor).astype(jnp.bfloat16)
            grads[1, :, cols] = (grad_key * factor).astype(jnp.bfloat16)
            grads[2, :, cols] = (grad_value * factor).astype(jnp.bfloat16)
        send_grads(g).start()

    for other in range(replicas):
        send_tokens(other, replica).wait_send()

    @pl.loop(0, groups)
    def _(g):
        for step in range(1, tensors):
            send_part(step, g).wait_send()
        send_out(g).wait()

    @pl.loop(0, groups)
    def _(g):
        send_grads(g).wait()


def on_device(fwd_qkv, fwd_segments, parked, bwd_segments, grad_out, loss_tokens):
    sections = lax.axis_size("pipe")
    tensors = lax.axis_size("tensor")
    replicas = lax.axis_size("dp")
    length, columns = fwd_qkv.shape[2], fwd_qkv.shape[3]
    groups = columns // (GROUP * HEAD_DIM)
    if sections > 2:
        grad_out = lax.ppermute(grad_out, "pipe", [(i, (-i) % sections) for i in range(sections)])
    dma = pltpu.SemaphoreType.DMA
    received, grads = pl.pallas_call(
        functools.partial(kernel, sections, tensors, replicas),
        out_shape=(
            jax.ShapeDtypeStruct((1, length, columns), jnp.bfloat16),
            jax.ShapeDtypeStruct((3, 1, length, columns), jnp.bfloat16),
        ),
        in_specs=[pl.BlockSpec(memory_space=pl.ANY)] * 6,
        out_specs=(pl.BlockSpec(memory_space=pl.ANY), pl.BlockSpec(memory_space=pl.ANY)),
        scratch_shapes=[
            pltpu.VMEM((3, length, columns), jnp.bfloat16),
            pltpu.VMEM((length, columns), jnp.bfloat16),
            pltpu.VMEM((3, length, columns), jnp.bfloat16),
            pltpu.VMEM((length, columns), jnp.bfloat16),
            pltpu.VMEM((3, length, columns), jnp.bfloat16),
            pltpu.VMEM((length, length), jnp.float32),
            pltpu.VMEM((length, length), jnp.float32),
            pltpu.VMEM((1, length), jnp.int32),
            pltpu.VMEM((1, length), jnp.int32),
            pltpu.SMEM((1,), jnp.int32),
            pltpu.VMEM((8, HEAD_DIM), jnp.int32),
            pltpu.VMEM((replicas, 8, HEAD_DIM), jnp.int32),
            dma((groups,)), dma((groups,)), dma((groups,)), dma((2,)),
            dma((tensors - 1, groups)), dma((tensors - 1, groups)),
            dma((groups,)), dma((groups,)), dma((groups,)), dma((groups,)),
            dma, dma, dma((replicas,)), dma((replicas,)),
        ],
        compiler_params=pltpu.CompilerParams(
            collective_id=0, has_side_effects=True, vmem_limit_bytes=48 * 1024 * 1024
        ),
        cost_estimate=pl.CostEstimate(
            flops=14 * length * length * columns, bytes_accessed=22 * length * columns, transcendentals=0
        ),
    )(fwd_qkv, fwd_segments, parked, bwd_segments, grad_out, loss_tokens)
    return received, grads


def solution(mesh):
    placed = (
        P(None, ("pipe", "dp"), None, "tensor"),
        P(("pipe", "dp"), None),
        P(None, ("pipe", "dp"), "tensor", None),
        P(("pipe", "dp"), None),
        P(("pipe", "dp"), None, "tensor"),
        P(("pipe", "dp")),
    )
    return jax.shard_map(
        on_device,
        mesh=mesh,
        in_specs=placed,
        out_specs=(P(("pipe", "dp"), None, "tensor"), P(None, ("pipe", "dp"), None, "tensor")),
        check_vma=False,
    )
```

```python
import functools

import jax
import jax.numpy as jnp
from jax import lax
from jax.experimental import pallas as pl
from jax.experimental.pallas import tpu as pltpu
from jax.sharding import PartitionSpec as P

HEAD_DIM = 128
SCALE = HEAD_DIM ** (-0.5)
GROUP = 2
AHEAD = 2
MESH = pl.DeviceIdType.MESH


def dot(a, b, contract):
    return lax.dot_general(a, b, (contract, ((), ())), preferred_element_type=jnp.float32)


def softmax(query, key, bias):
    logits = dot(query, key, ((1,), (1,))) * SCALE + bias
    weights = jnp.exp(logits - jnp.max(logits, axis=-1, keepdims=True))
    return weights / jnp.sum(weights, axis=-1, keepdims=True)


def mask_bias(segment):
    length = segment.shape[1]
    along = jnp.broadcast_to(segment.astype(jnp.float32), (length, length))
    return jnp.where(along == along.T, jnp.float32(0), jnp.float32(-1e30))


def kernel(
    sections, tensors, replicas,
    fwd_hbm, fwd_seg_hbm, parked_hbm, bwd_seg_hbm, up_hbm, tokens_hbm,
    received_hbm, grads_hbm,
    fwd, out, stash, up, grads, fwd_bias, bwd_bias, fwd_seg, bwd_seg, tokens, token_tile, token_all,
    fwd_sem, up_sem, own_sem, small_sem,
    part_send, part_recv, out_send, out_recv, grad_send, grad_recv,
    seg_send, seg_recv, tok_send, tok_recv,
):
    section = lax.axis_index("pipe")
    lane = lax.axis_index("tensor")
    replica = lax.axis_index("dp")
    after = lax.rem(section + 1, sections)
    before = lax.rem(section + sections - 1, sections)
    mirror = sections - 1 - section
    length = fwd.shape[1]
    width = GROUP * HEAD_DIM
    columns = fwd.shape[2]
    groups = columns // width
    rows = parked_hbm.shape[2]

    barrier = pltpu.get_barrier_semaphore()
    greeted = 0
    for step in range(1, tensors):
        pl.semaphore_signal(barrier, inc=1, device_id={"tensor": lax.rem(lane + step, tensors)}, device_id_type=MESH)
        greeted += 1
    for other in range(replicas):
        pl.semaphore_signal(barrier, inc=1, device_id={"pipe": mirror, "dp": other}, device_id_type=MESH)
        greeted += 1
    if sections > 2:
        for other in (after, before):
            pl.semaphore_signal(barrier, inc=1, device_id={"pipe": other}, device_id_type=MESH)
            greeted += 1

    def span(g):
        return pl.ds(pl.multiple_of(g * width, width), width)

    def load_fwd(g):
        return pltpu.make_async_copy(fwd_hbm.at[:, 0, :, span(g)], fwd.at[:, :, span(g)], fwd_sem.at[g])

    def load_up(g):
        return pltpu.make_async_copy(up_hbm.at[0, :, span(g)], up.at[:, span(g)], up_sem.at[g])

    def my_rows(who):
        return pl.ds(pl.multiple_of(who * rows, rows), rows)

    def parked_span(who, g):
        return pl.ds(pl.multiple_of(who * columns + g * width, width), width)

    def load_own(g):
        return pltpu.make_async_copy(
            parked_hbm.at[:, 0, :, parked_span(lane, g)], stash.at[:, my_rows(lane), span(g)], own_sem.at[g]
        )

    def send_part(step, g):
        other = lax.rem(lane + step, tensors)
        return pltpu.make_async_remote_copy(
            src_ref=parked_hbm.at[:, 0, :, parked_span(other, g)],
            dst_ref=stash.at[:, my_rows(lane), span(g)],
            send_sem=part_send.at[step - 1, g],
            recv_sem=part_recv.at[step - 1, g],
            device_id={"tensor": other},
            device_id_type=MESH,
        )

    def recv_part(step, g):
        other = lax.rem(lane + tensors - step, tensors)
        return pltpu.make_async_remote_copy(
            src_ref=parked_hbm.at[:, 0, :, parked_span(lane, g)],
            dst_ref=stash.at[:, my_rows(other), span(g)],
            send_sem=part_send.at[step - 1, g],
            recv_sem=part_recv.at[step - 1, g],
            device_id={"tensor": other},
            device_id_type=MESH,
        )

    def send_out(g):
        return pltpu.make_async_remote_copy(
            src_ref=out.at[:, span(g)],
            dst_ref=received_hbm.at[0, :, span(g)],
            send_sem=out_send.at[g],
            recv_sem=out_recv.at[g],
            device_id={"pipe": after},
            device_id_type=MESH,
        )

    def send_grads(g):
        return pltpu.make_async_remote_copy(
            src_ref=grads.at[:, :, span(g)],
            dst_ref=grads_hbm.at[:, 0, :, span(g)],
            send_sem=grad_send.at[g],
            recv_sem=grad_recv.at[g],
            device_id={"pipe": mirror},
            device_id_type=MESH,
        )

    def send_tokens(other, mine):
        return pltpu.make_async_remote_copy(
            src_ref=token_tile,
            dst_ref=token_all.at[mine],
            send_sem=tok_send.at[other],
            recv_sem=tok_recv.at[mine],
            device_id={"pipe": mirror, "dp": other},
            device_id_type=MESH,
        )

    send_segment = pltpu.make_async_remote_copy(
        src_ref=bwd_seg_hbm,
        dst_ref=bwd_seg,
        send_sem=seg_send,
        recv_sem=seg_recv,
        device_id={"pipe": mirror},
        device_id_type=MESH,
    )

    seg_copy = pltpu.make_async_copy(fwd_seg_hbm, fwd_seg, small_sem.at[0])
    tok_copy = pltpu.make_async_copy(tokens_hbm, tokens, small_sem.at[1])
    seg_copy.start()
    tok_copy.start()
    pl.loop(0, groups)(lambda g: load_fwd(g).start())
    pl.loop(0, groups)(lambda g: load_own(g).start())
    pl.loop(0, groups)(lambda g: load_up(g).start())

    def forward(g):
        load_fwd(g).wait()
        for h in range(GROUP):
            cols = pl.ds(pl.multiple_of(g * width + h * HEAD_DIM, HEAD_DIM), HEAD_DIM)
            probs = softmax(fwd[0, :, cols], fwd[1, :, cols], fwd_bias[...])
            mixed = dot(probs.astype(jnp.bfloat16), fwd[2, :, cols], ((1,), (0,)))
            out[:, cols] = mixed.astype(jnp.bfloat16)

    tok_copy.wait()
    token_tile[...] = jnp.full(token_tile.shape, tokens[0], jnp.int32)

    seg_copy.wait()
    fwd_bias[...] = mask_bias(fwd_seg[...])
    forward(0)

    pl.semaphore_wait(barrier, greeted)
    send_out(0).start()
    send_segment.start()
    for other in range(replicas):
        send_tokens(other, replica).start()

    def exchange(g):
        for step in range(1, tensors):
            send_part(step, g).start()

    for g in range(AHEAD):
        exchange(g)

    @pl.loop(1, groups)
    def _(g):
        forward(g)
        send_out(g).start()

    send_segment.wait()
    bwd_bias[...] = mask_bias(bwd_seg[...])
    total = jnp.zeros((1, HEAD_DIM), jnp.float32)
    for other in range(replicas):
        send_tokens(other, other).wait_recv()
        total += token_all[other, 0:1, :].astype(jnp.float32)
    factor = jnp.float32(replicas * length) / total

    @pl.loop(0, groups)
    def _(g):
        load_own(g).wait()
        load_up(g).wait()
        for step in range(1, tensors):
            recv_part(step, g).wait_recv()

        @pl.when(g < groups - AHEAD)
        def _():
            exchange(g + AHEAD)

        for h in range(GROUP):
            cols = pl.ds(pl.multiple_of(g * width + h * HEAD_DIM, HEAD_DIM), HEAD_DIM)
            query, key, value, upstream = stash[0, :, cols], stash[1, :, cols], stash[2, :, cols], up[:, cols]
            probs = softmax(query, key, bwd_bias[...])
            grad_value = dot(probs.astype(jnp.bfloat16), upstream, ((0,), (0,)))
            grad_probs = dot(upstream, value, ((1,), (1,)))
            center = jnp.sum(probs * grad_probs, axis=-1, keepdims=True)
            grad_logits = (probs * (grad_probs - center) * SCALE).astype(jnp.bfloat16)
            grad_query = dot(grad_logits, key, ((1,), (0,)))
            grad_key = dot(grad_logits, query, ((0,), (0,)))
            grads[0, :, cols] = (grad_query * factor).astype(jnp.bfloat16)
            grads[1, :, cols] = (grad_key * factor).astype(jnp.bfloat16)
            grads[2, :, cols] = (grad_value * factor).astype(jnp.bfloat16)
        send_grads(g).start()

    for other in range(replicas):
        send_tokens(other, replica).wait_send()

    @pl.loop(0, groups)
    def _(g):
        for step in range(1, tensors):
            send_part(step, g).wait_send()
        send_out(g).wait()

    @pl.loop(0, groups)
    def _(g):
        send_grads(g).wait()


def on_device(fwd_qkv, fwd_segments, parked, bwd_segments, grad_out, loss_tokens):
    sections = lax.axis_size("pipe")
    tensors = lax.axis_size("tensor")
    replicas = lax.axis_size("dp")
    length, columns = fwd_qkv.shape[2], fwd_qkv.shape[3]
    groups = columns // (GROUP * HEAD_DIM)
    if sections > 2:
        grad_out = lax.ppermute(grad_out, "pipe", [(i, (-i) % sections) for i in range(sections)])
    dma = pltpu.SemaphoreType.DMA
    received, grads = pl.pallas_call(
        functools.partial(kernel, sections, tensors, replicas),
        out_shape=(
            jax.ShapeDtypeStruct((1, length, columns), jnp.bfloat16),
            jax.ShapeDtypeStruct((3, 1, length, columns), jnp.bfloat16),
        ),
        in_specs=[pl.BlockSpec(memory_space=pltpu.HBM)] * 6,
        out_specs=(pl.BlockSpec(memory_space=pl.ANY), pl.BlockSpec(memory_space=pl.ANY)),
        scratch_shapes=[
            pltpu.VMEM((3, length, columns), jnp.bfloat16),
            pltpu.VMEM((length, columns), jnp.bfloat16),
            pltpu.VMEM((3, length, columns), jnp.bfloat16),
            pltpu.VMEM((length, columns), jnp.bfloat16),
            pltpu.VMEM((3, length, columns), jnp.bfloat16),
            pltpu.VMEM((length, length), jnp.float32),
            pltpu.VMEM((length, length), jnp.float32),
            pltpu.VMEM((1, length), jnp.int32),
            pltpu.VMEM((1, length), jnp.int32),
            pltpu.SMEM((1,), jnp.int32),
            pltpu.VMEM((8, HEAD_DIM), jnp.int32),
            pltpu.VMEM((replicas, 8, HEAD_DIM), jnp.int32),
            dma((groups,)), dma((groups,)), dma((groups,)), dma((2,)),
            dma((tensors - 1, groups)), dma((tensors - 1, groups)),
            dma((groups,)), dma((groups,)), dma((groups,)), dma((groups,)),
            dma, dma, dma((replicas,)), dma((replicas,)),
        ],
        compiler_params=pltpu.CompilerParams(
            collective_id=0, has_side_effects=True, vmem_limit_bytes=48 * 1024 * 1024
        ),
        cost_estimate=pl.CostEstimate(
            flops=14 * length * length * columns, bytes_accessed=22 * length * columns, transcendentals=0
        ),
    )(fwd_qkv, fwd_segments, parked, bwd_segments, grad_out, loss_tokens)
    return received, grads


def solution(mesh):
    placed = (
        P(None, ("pipe", "dp"), None, "tensor"),
        P(("pipe", "dp"), None),
        P(None, ("pipe", "dp"), "tensor", None),
        P(("pipe", "dp"), None),
        P(("pipe", "dp"), None, "tensor"),
        P(("pipe", "dp")),
    )
    return jax.shard_map(
        on_device,
        mesh=mesh,
        in_specs=placed,
        out_specs=(P(("pipe", "dp"), None, "tensor"), P(None, ("pipe", "dp"), None, "tensor")),
        check_vma=False,
    )
```

```python
import functools

import jax
import jax.numpy as jnp
from jax import lax
from jax.experimental import pallas as pl
from jax.experimental.pallas import tpu as pltpu
from jax.sharding import PartitionSpec as P

HEAD_DIM = 128
SCALE = HEAD_DIM ** (-0.5)
GROUP = 2
AHEAD = 2
MESH = pl.DeviceIdType.MESH


def dot(a, b, contract):
    return lax.dot_general(a, b, (contract, ((), ())), preferred_element_type=jnp.float32)


def softmax(query, key, bias):
    logits = dot(query, key, ((1,), (1,))) * SCALE + bias
    weights = jnp.exp(logits - jnp.max(logits, axis=-1, keepdims=True))
    return weights / jnp.sum(weights, axis=-1, keepdims=True)


def mask_bias(segment):
    length = segment.shape[1]
    along = jnp.broadcast_to(segment.astype(jnp.float32), (length, length))
    return jnp.where(along == along.T, jnp.float32(0), jnp.float32(-1e30))


def kernel(
    sections, tensors, replicas,
    fwd_hbm, fwd_seg_hbm, parked_hbm, bwd_seg_hbm, up_hbm, tokens_hbm,
    received_hbm, grads_hbm,
    fwd, out, stash, up, grads, fwd_bias, bwd_bias, fwd_seg, bwd_seg, tokens, token_tile, token_all,
    fwd_sem, up_sem, own_sem, small_sem,
    part_send, part_recv, out_send, out_recv, grad_send, grad_recv,
    seg_send, seg_recv, tok_send, tok_recv,
):
    section = lax.axis_index("pipe")
    lane = lax.axis_index("tensor")
    replica = lax.axis_index("dp")
    after = lax.rem(section + 1, sections)
    before = lax.rem(section + sections - 1, sections)
    mirror = sections - 1 - section
    length = fwd.shape[1]
    width = GROUP * HEAD_DIM
    columns = fwd.shape[2]
    groups = columns // width
    rows = parked_hbm.shape[2]

    barrier = pltpu.get_barrier_semaphore()
    greeted = 0
    for step in range(1, tensors):
        pl.semaphore_signal(barrier, inc=1, device_id={"tensor": lax.rem(lane + step, tensors)}, device_id_type=MESH)
        greeted += 1
    for other in range(replicas):
        pl.semaphore_signal(barrier, inc=1, device_id={"pipe": mirror, "dp": other}, device_id_type=MESH)
        greeted += 1
    if sections > 2:
        for other in (after, before):
            pl.semaphore_signal(barrier, inc=1, device_id={"pipe": other}, device_id_type=MESH)
            greeted += 1

    def span(g):
        return pl.ds(pl.multiple_of(g * width, width), width)

    def load_fwd(g):
        return pltpu.make_async_copy(fwd_hbm.at[:, 0, :, span(g)], fwd.at[:, :, span(g)], fwd_sem.at[g])

    def load_up(g):
        return pltpu.make_async_copy(up_hbm.at[0, :, span(g)], up.at[:, span(g)], up_sem.at[g])

    def my_rows(who):
        return pl.ds(pl.multiple_of(who * rows, rows), rows)

    def parked_span(who, g):
        return pl.ds(pl.multiple_of(who * columns + g * width, width), width)

    def load_own(g):
        return pltpu.make_async_copy(
            parked_hbm.at[:, 0, :, parked_span(lane, g)], stash.at[:, my_rows(lane), span(g)], own_sem.at[g]
        )

    def send_part(step, g):
        other = lax.rem(lane + step, tensors)
        return pltpu.make_async_remote_copy(
            src_ref=parked_hbm.at[:, 0, :, parked_span(other, g)],
            dst_ref=stash.at[:, my_rows(lane), span(g)],
            send_sem=part_send.at[step - 1, g],
            recv_sem=part_recv.at[step - 1, g],
            device_id={"tensor": other},
            device_id_type=MESH,
        )

    def recv_part(step, g):
        other = lax.rem(lane + tensors - step, tensors)
        return pltpu.make_async_remote_copy(
            src_ref=parked_hbm.at[:, 0, :, parked_span(lane, g)],
            dst_ref=stash.at[:, my_rows(other), span(g)],
            send_sem=part_send.at[step - 1, g],
            recv_sem=part_recv.at[step - 1, g],
            device_id={"tensor": other},
            device_id_type=MESH,
        )

    def send_out(g):
        return pltpu.make_async_remote_copy(
            src_ref=out.at[:, span(g)],
            dst_ref=received_hbm.at[0, :, span(g)],
            send_sem=out_send.at[g],
            recv_sem=out_recv.at[g],
            device_id={"pipe": after},
            device_id_type=MESH,
        )

    def send_grads(g):
        return pltpu.make_async_remote_copy(
            src_ref=grads.at[:, :, span(g)],
            dst_ref=grads_hbm.at[:, 0, :, span(g)],
            send_sem=grad_send.at[g],
            recv_sem=grad_recv.at[g],
            device_id={"pipe": mirror},
            device_id_type=MESH,
        )

    def send_tokens(other, mine):
        return pltpu.make_async_remote_copy(
            src_ref=token_tile,
            dst_ref=token_all.at[mine],
            send_sem=tok_send.at[other],
            recv_sem=tok_recv.at[mine],
            device_id={"pipe": mirror, "dp": other},
            device_id_type=MESH,
        )

    send_segment = pltpu.make_async_remote_copy(
        src_ref=bwd_seg_hbm,
        dst_ref=bwd_seg,
        send_sem=seg_send,
        recv_sem=seg_recv,
        device_id={"pipe": mirror},
        device_id_type=MESH,
    )

    seg_copy = pltpu.make_async_copy(fwd_seg_hbm, fwd_seg, small_sem.at[0])
    tok_copy = pltpu.make_async_copy(tokens_hbm, tokens, small_sem.at[1])
    seg_copy.start()
    tok_copy.start()
    pl.loop(0, groups)(lambda g: load_fwd(g).start())
    pl.loop(0, groups)(lambda g: load_own(g).start())
    pl.loop(0, groups)(lambda g: load_up(g).start())

    def forward(g):
        load_fwd(g).wait()
        for h in range(GROUP):
            cols = pl.ds(pl.multiple_of(g * width + h * HEAD_DIM, HEAD_DIM), HEAD_DIM)
            probs = softmax(fwd[0, :, cols], fwd[1, :, cols], fwd_bias[...])
            mixed = dot(probs.astype(jnp.bfloat16), fwd[2, :, cols], ((1,), (0,)))
            out[:, cols] = mixed.astype(jnp.bfloat16)

    tok_copy.wait()
    token_tile[...] = jnp.full(token_tile.shape, tokens[0], jnp.int32)

    seg_copy.wait()
    fwd_bias[...] = mask_bias(fwd_seg[...])
    forward(0)

    pl.semaphore_wait(barrier, greeted)
    send_out(0).start()
    send_segment.start()
    for other in range(replicas):
        send_tokens(other, replica).start()

    def exchange(g):
        for step in range(1, tensors):
            send_part(step, g).start()

    for g in range(AHEAD):
        exchange(g)

    @pl.loop(1, groups)
    def _(g):
        forward(g)
        send_out(g).start()

    send_segment.wait()
    bwd_bias[...] = mask_bias(bwd_seg[...])
    total = jnp.zeros((1, HEAD_DIM), jnp.float32)
    for other in range(replicas):
        send_tokens(other, other).wait_recv()
        total += token_all[other, 0:1, :].astype(jnp.float32)
    factor = jnp.float32(replicas * length) / total

    @pl.loop(0, groups)
    def _(g):
        load_own(g).wait()
        load_up(g).wait()
        for step in range(1, tensors):
            recv_part(step, g).wait_recv()

        @pl.when(g < groups - AHEAD)
        def _():
            exchange(g + AHEAD)

        for h in range(GROUP):
            cols = pl.ds(pl.multiple_of(g * width + h * HEAD_DIM, HEAD_DIM), HEAD_DIM)
            query, key, value, upstream = stash[0, :, cols], stash[1, :, cols], stash[2, :, cols], up[:, cols]
            probs = softmax(query, key, bwd_bias[...])
            grad_value = dot(probs.astype(jnp.bfloat16), upstream, ((0,), (0,)))
            grad_probs = dot(upstream, value, ((1,), (1,)))
            center = jnp.sum(probs * grad_probs, axis=-1, keepdims=True)
            grad_logits = (probs * (grad_probs - center) * SCALE).astype(jnp.bfloat16)
            grad_query = dot(grad_logits, key, ((1,), (0,)))
            grad_key = dot(grad_logits, query, ((0,), (0,)))
            grads[0, :, cols] = (grad_query * factor).astype(jnp.bfloat16)
            grads[1, :, cols] = (grad_key * factor).astype(jnp.bfloat16)
            grads[2, :, cols] = (grad_value * factor).astype(jnp.bfloat16)
        send_grads(g).start()

    for other in range(replicas):
        send_tokens(other, replica).wait_send()

    @pl.loop(0, groups)
    def _(g):
        for step in range(1, tensors):
            send_part(step, g).wait_send()
        send_out(g).wait()

    @pl.loop(0, groups)
    def _(g):
        send_grads(g).wait()


def on_device(fwd_qkv, fwd_segments, parked, bwd_segments, grad_out, loss_tokens):
    sections = lax.axis_size("pipe")
    tensors = lax.axis_size("tensor")
    replicas = lax.axis_size("dp")
    length, columns = fwd_qkv.shape[2], fwd_qkv.shape[3]
    groups = columns // (GROUP * HEAD_DIM)
    if sections > 2:
        grad_out = lax.ppermute(grad_out, "pipe", [(i, (-i) % sections) for i in range(sections)])
    dma = pltpu.SemaphoreType.DMA
    received, grads = pl.pallas_call(
        functools.partial(kernel, sections, tensors, replicas),
        out_shape=(
            jax.ShapeDtypeStruct((1, length, columns), jnp.bfloat16),
            jax.ShapeDtypeStruct((3, 1, length, columns), jnp.bfloat16),
        ),
        in_specs=[pl.BlockSpec(memory_space=pltpu.HBM)] * 6,
        out_specs=(pl.BlockSpec(memory_space=pl.ANY), pl.BlockSpec(memory_space=pl.ANY)),
        scratch_shapes=[
            pltpu.VMEM((3, length, columns), jnp.bfloat16),
            pltpu.VMEM((length, columns), jnp.bfloat16),
            pltpu.VMEM((3, length, columns), jnp.bfloat16),
            pltpu.VMEM((length, columns), jnp.bfloat16),
            pltpu.VMEM((3, length, columns), jnp.bfloat16),
            pltpu.VMEM((length, length), jnp.float32),
            pltpu.VMEM((length, length), jnp.float32),
            pltpu.VMEM((1, length), jnp.int32),
            pltpu.VMEM((1, length), jnp.int32),
            pltpu.SMEM((1,), jnp.int32),
            pltpu.VMEM((8, HEAD_DIM), jnp.int32),
            pltpu.VMEM((replicas, 8, HEAD_DIM), jnp.int32),
            dma((groups,)), dma((groups,)), dma((groups,)), dma((2,)),
            dma((tensors - 1, groups)), dma((tensors - 1, groups)),
            dma((groups,)), dma((groups,)), dma((groups,)), dma((groups,)),
            dma, dma, dma((replicas,)), dma((replicas,)),
        ],
        compiler_params=pltpu.CompilerParams(
            collective_id=0, has_side_effects=True, vmem_limit_bytes=48 * 1024 * 1024
        ),
        cost_estimate=pl.CostEstimate(
            flops=14 * length * length * columns, bytes_accessed=22 * length * columns, transcendentals=0
        ),
    )(*(pltpu.with_memory_space_constraint(x, pltpu.HBM) for x in (fwd_qkv, fwd_segments, parked, bwd_segments, grad_out)), loss_tokens)
    return received, grads


def solution(mesh):
    placed = (
        P(None, ("pipe", "dp"), None, "tensor"),
        P(("pipe", "dp"), None),
        P(None, ("pipe", "dp"), "tensor", None),
        P(("pipe", "dp"), None),
        P(("pipe", "dp"), None, "tensor"),
        P(("pipe", "dp")),
    )
    return jax.shard_map(
        on_device,
        mesh=mesh,
        in_specs=placed,
        out_specs=(P(("pipe", "dp"), None, "tensor"), P(None, ("pipe", "dp"), None, "tensor")),
        check_vma=False,
    )
```

```python
import functools

import jax
import jax.numpy as jnp
from jax import lax
from jax.experimental import pallas as pl
from jax.experimental.pallas import tpu as pltpu
from jax.sharding import PartitionSpec as P

HEAD_DIM = 128
SCALE = HEAD_DIM ** (-0.5)
GROUP = 2
AHEAD = 2
MESH = pl.DeviceIdType.MESH


def dot(a, b, contract):
    return lax.dot_general(a, b, (contract, ((), ())), preferred_element_type=jnp.float32)


def softmax(query, key, bias):
    logits = dot(query, key, ((1,), (1,))) * SCALE + bias
    weights = jnp.exp(logits - jnp.max(logits, axis=-1, keepdims=True))
    return weights / jnp.sum(weights, axis=-1, keepdims=True)


def mask_bias(segment):
    length = segment.shape[1]
    along = jnp.broadcast_to(segment.astype(jnp.float32), (length, length))
    return jnp.where(along == along.T, jnp.float32(0), jnp.float32(-1e30))


def kernel(
    sections, tensors, replicas,
    fwd_hbm, fwd_seg_hbm, parked_hbm, bwd_seg_hbm, up_hbm, tokens_hbm,
    received_hbm, grads_hbm,
    fwd, out, stash, up, grads, fwd_bias, bwd_bias, fwd_seg, bwd_seg, tokens, token_tile, token_all,
    fwd_sem, up_sem, own_sem, small_sem,
    part_send, part_recv, out_send, out_recv, grad_send, grad_recv,
    seg_send, seg_recv, tok_send, tok_recv,
):
    section = lax.axis_index("pipe")
    lane = lax.axis_index("tensor")
    replica = lax.axis_index("dp")
    after = lax.rem(section + 1, sections)
    before = lax.rem(section + sections - 1, sections)
    mirror = sections - 1 - section
    length = fwd.shape[1]
    width = GROUP * HEAD_DIM
    columns = fwd.shape[2]
    groups = columns // width
    rows = parked_hbm.shape[2]

    barrier = pltpu.get_barrier_semaphore()
    greeted = 0
    for step in range(1, tensors):
        pl.semaphore_signal(barrier, inc=1, device_id={"tensor": lax.rem(lane + step, tensors)}, device_id_type=MESH)
        greeted += 1
    for other in range(replicas):
        pl.semaphore_signal(barrier, inc=1, device_id={"pipe": mirror, "dp": other}, device_id_type=MESH)
        greeted += 1
    if sections > 2:
        for other in (after, before):
            pl.semaphore_signal(barrier, inc=1, device_id={"pipe": other}, device_id_type=MESH)
            greeted += 1

    def span(g):
        return pl.ds(pl.multiple_of(g * width, width), width)

    def load_fwd(g):
        return pltpu.make_async_copy(fwd_hbm.at[:, 0, :, span(g)], fwd.at[:, :, span(g)], fwd_sem.at[g])

    def load_up(g):
        return pltpu.make_async_copy(up_hbm.at[0, :, span(g)], up.at[:, span(g)], up_sem.at[g])

    def my_rows(who):
        return pl.ds(pl.multiple_of(who * rows, rows), rows)

    def parked_span(who, g):
        return pl.ds(pl.multiple_of(who * columns + g * width, width), width)

    def load_own(g):
        return pltpu.make_async_copy(
            parked_hbm.at[:, 0, :, parked_span(lane, g)], stash.at[:, my_rows(lane), span(g)], own_sem.at[g]
        )

    def send_part(step, g):
        other = lax.rem(lane + step, tensors)
        return pltpu.make_async_remote_copy(
            src_ref=parked_hbm.at[:, 0, :, parked_span(other, g)],
            dst_ref=stash.at[:, my_rows(lane), span(g)],
            send_sem=part_send.at[step - 1, g],
            recv_sem=part_recv.at[step - 1, g],
            device_id={"tensor": other},
            device_id_type=MESH,
        )

    def recv_part(step, g):
        other = lax.rem(lane + tensors - step, tensors)
        return pltpu.make_async_remote_copy(
            src_ref=parked_hbm.at[:, 0, :, parked_span(lane, g)],
            dst_ref=stash.at[:, my_rows(other), span(g)],
            send_sem=part_send.at[step - 1, g],
            recv_sem=part_recv.at[step - 1, g],
            device_id={"tensor": other},
            device_id_type=MESH,
        )

    def send_out(g):
        return pltpu.make_async_remote_copy(
            src_ref=out.at[:, span(g)],
            dst_ref=received_hbm.at[0, :, span(g)],
            send_sem=out_send.at[g],
            recv_sem=out_recv.at[g],
            device_id={"pipe": after},
            device_id_type=MESH,
        )

    def send_grads(g):
        return pltpu.make_async_remote_copy(
            src_ref=grads.at[:, :, span(g)],
            dst_ref=grads_hbm.at[:, 0, :, span(g)],
            send_sem=grad_send.at[g],
            recv_sem=grad_recv.at[g],
            device_id={"pipe": mirror},
            device_id_type=MESH,
        )

    def send_tokens(other, mine):
        return pltpu.make_async_remote_copy(
            src_ref=token_tile,
            dst_ref=token_all.at[mine],
            send_sem=tok_send.at[other],
            recv_sem=tok_recv.at[mine],
            device_id={"pipe": mirror, "dp": other},
            device_id_type=MESH,
        )

    send_segment = pltpu.make_async_remote_copy(
        src_ref=bwd_seg_hbm,
        dst_ref=bwd_seg,
        send_sem=seg_send,
        recv_sem=seg_recv,
        device_id={"pipe": mirror},
        device_id_type=MESH,
    )

    seg_copy = pltpu.make_async_copy(fwd_seg_hbm, fwd_seg, small_sem.at[0])
    tok_copy = pltpu.make_async_copy(tokens_hbm, tokens, small_sem.at[1])
    seg_copy.start()
    tok_copy.start()
    pl.loop(0, groups)(lambda g: load_fwd(g).start())
    pl.loop(0, groups)(lambda g: load_own(g).start())
    pl.loop(0, groups)(lambda g: load_up(g).start())

    def forward(g):
        load_fwd(g).wait()
        for h in range(GROUP):
            cols = pl.ds(pl.multiple_of(g * width + h * HEAD_DIM, HEAD_DIM), HEAD_DIM)
            probs = softmax(fwd[0, :, cols], fwd[1, :, cols], fwd_bias[...])
            mixed = dot(probs.astype(jnp.bfloat16), fwd[2, :, cols], ((1,), (0,)))
            out[:, cols] = mixed.astype(jnp.bfloat16)

    tok_copy.wait()
    token_tile[...] = jnp.full(token_tile.shape, tokens[0], jnp.int32)

    seg_copy.wait()
    fwd_bias[...] = mask_bias(fwd_seg[...])
    forward(0)

    pl.semaphore_wait(barrier, greeted)
    send_out(0).start()
    send_segment.start()
    for other in range(replicas):
        send_tokens(other, replica).start()

    def exchange(g):
        for step in range(1, tensors):
            send_part(step, g).start()

    for g in range(AHEAD):
        exchange(g)

    @pl.loop(1, groups)
    def _(g):
        forward(g)
        send_out(g).start()

    send_segment.wait()
    bwd_bias[...] = mask_bias(bwd_seg[...])
    total = jnp.zeros((1, HEAD_DIM), jnp.float32)
    for other in range(replicas):
        send_tokens(other, other).wait_recv()
        total += token_all[other, 0:1, :].astype(jnp.float32)
    factor = jnp.float32(replicas * length) / total

    @pl.loop(0, groups)
    def _(g):
        load_own(g).wait()
        load_up(g).wait()
        for step in range(1, tensors):
            recv_part(step, g).wait_recv()

        @pl.when(g < groups - AHEAD)
        def _():
            exchange(g + AHEAD)

        for h in range(GROUP):
            cols = pl.ds(pl.multiple_of(g * width + h * HEAD_DIM, HEAD_DIM), HEAD_DIM)
            query, key, value, upstream = stash[0, :, cols], stash[1, :, cols], stash[2, :, cols], up[:, cols]
            probs = softmax(query, key, bwd_bias[...])
            grad_value = dot(probs.astype(jnp.bfloat16), upstream, ((0,), (0,)))
            grad_probs = dot(upstream, value, ((1,), (1,)))
            center = jnp.sum(probs * grad_probs, axis=-1, keepdims=True)
            grad_logits = (probs * (grad_probs - center) * SCALE).astype(jnp.bfloat16)
            grad_query = dot(grad_logits, key, ((1,), (0,)))
            grad_key = dot(grad_logits, query, ((0,), (0,)))
            grads[0, :, cols] = (grad_query * factor).astype(jnp.bfloat16)
            grads[1, :, cols] = (grad_key * factor).astype(jnp.bfloat16)
            grads[2, :, cols] = (grad_value * factor).astype(jnp.bfloat16)
        send_grads(g).start()

    for other in range(replicas):
        send_tokens(other, replica).wait_send()

    @pl.loop(0, groups)
    def _(g):
        for step in range(1, tensors):
            send_part(step, g).wait_send()
        send_out(g).wait()

    @pl.loop(0, groups)
    def _(g):
        send_grads(g).wait()


def store(received, grads, received_out, grads_out, sems):
    copies = [pltpu.make_async_copy(received, received_out, sems.at[0])]
    for k in range(3):
        copies.append(pltpu.make_async_copy(grads.at[k], grads_out.at[k], sems.at[1 + k]))
    for copy in copies:
        copy.start()
    for copy in copies:
        copy.wait()


def on_device(fwd_qkv, fwd_segments, parked, bwd_segments, grad_out, loss_tokens):
    sections = lax.axis_size("pipe")
    tensors = lax.axis_size("tensor")
    replicas = lax.axis_size("dp")
    length, columns = fwd_qkv.shape[2], fwd_qkv.shape[3]
    groups = columns // (GROUP * HEAD_DIM)
    if sections > 2:
        grad_out = lax.ppermute(grad_out, "pipe", [(i, (-i) % sections) for i in range(sections)])
    dma = pltpu.SemaphoreType.DMA
    received, grads = pl.pallas_call(
        functools.partial(kernel, sections, tensors, replicas),
        out_shape=(
            jax.ShapeDtypeStruct((1, length, columns), jnp.bfloat16),
            jax.ShapeDtypeStruct((3, 1, length, columns), jnp.bfloat16),
        ),
        in_specs=[pl.BlockSpec(memory_space=pltpu.HBM)] * 6,
        out_specs=(pl.BlockSpec(memory_space=pl.ANY), pl.BlockSpec(memory_space=pl.ANY)),
        scratch_shapes=[
            pltpu.VMEM((3, length, columns), jnp.bfloat16),
            pltpu.VMEM((length, columns), jnp.bfloat16),
            pltpu.VMEM((3, length, columns), jnp.bfloat16),
            pltpu.VMEM((length, columns), jnp.bfloat16),
            pltpu.VMEM((3, length, columns), jnp.bfloat16),
            pltpu.VMEM((length, length), jnp.float32),
            pltpu.VMEM((length, length), jnp.float32),
            pltpu.VMEM((1, length), jnp.int32),
            pltpu.VMEM((1, length), jnp.int32),
            pltpu.SMEM((1,), jnp.int32),
            pltpu.VMEM((8, HEAD_DIM), jnp.int32),
            pltpu.VMEM((replicas, 8, HEAD_DIM), jnp.int32),
            dma((groups,)), dma((groups,)), dma((groups,)), dma((2,)),
            dma((tensors - 1, groups)), dma((tensors - 1, groups)),
            dma((groups,)), dma((groups,)), dma((groups,)), dma((groups,)),
            dma, dma, dma((replicas,)), dma((replicas,)),
        ],
        compiler_params=pltpu.CompilerParams(
            collective_id=0, has_side_effects=True, vmem_limit_bytes=48 * 1024 * 1024
        ),
        cost_estimate=pl.CostEstimate(
            flops=14 * length * length * columns, bytes_accessed=22 * length * columns, transcendentals=0
        ),
    )(*(pltpu.with_memory_space_constraint(x, pltpu.HBM) for x in (fwd_qkv, fwd_segments, parked, bwd_segments, grad_out)), loss_tokens)
    return pl.pallas_call(
        store,
        out_shape=(
            jax.ShapeDtypeStruct(received.shape, jnp.bfloat16),
            jax.ShapeDtypeStruct(grads.shape, jnp.bfloat16),
        ),
        in_specs=[pl.BlockSpec(memory_space=pl.ANY)] * 2,
        out_specs=(pl.BlockSpec(memory_space=pl.ANY), pl.BlockSpec(memory_space=pl.ANY)),
        scratch_shapes=[dma((4,))],
    )(received, grads)


def solution(mesh):
    placed = (
        P(None, ("pipe", "dp"), None, "tensor"),
        P(("pipe", "dp"), None),
        P(None, ("pipe", "dp"), "tensor", None),
        P(("pipe", "dp"), None),
        P(("pipe", "dp"), None, "tensor"),
        P(("pipe", "dp")),
    )
    return jax.shard_map(
        on_device,
        mesh=mesh,
        in_specs=placed,
        out_specs=(P(("pipe", "dp"), None, "tensor"), P(None, ("pipe", "dp"), None, "tensor")),
        check_vma=False,
    )
```

```python
import functools

import jax
import jax.numpy as jnp
from jax import lax
from jax.experimental import pallas as pl
from jax.experimental.pallas import tpu as pltpu
from jax.sharding import PartitionSpec as P

HEAD_DIM = 128
SCALE = HEAD_DIM ** (-0.5)
GROUP = 2
AHEAD = 2
MESH = pl.DeviceIdType.MESH


def dot(a, b, contract):
    return lax.dot_general(a, b, (contract, ((), ())), preferred_element_type=jnp.float32)


def softmax(query, key, bias):
    logits = dot(query, key, ((1,), (1,))) * SCALE + bias
    weights = jnp.exp(logits - jnp.max(logits, axis=-1, keepdims=True))
    return weights / jnp.sum(weights, axis=-1, keepdims=True)


def mask_bias(segment):
    length = segment.shape[1]
    along = jnp.broadcast_to(segment.astype(jnp.float32), (length, length))
    return jnp.where(along == along.T, jnp.float32(0), jnp.float32(-1e30))


def kernel(
    sections, tensors, replicas,
    fwd_hbm, fwd_seg_hbm, parked_hbm, bwd_seg_hbm, up_hbm, tokens_hbm,
    received_hbm, grads_hbm,
    fwd, out, stash, up, grads, fwd_bias, bwd_bias, fwd_seg, bwd_seg, tokens, token_tile, token_all,
    fwd_sem, up_sem, own_sem, small_sem,
    part_send, part_recv, out_send, out_recv, grad_send, grad_recv,
    seg_send, seg_recv, tok_send, tok_recv,
):
    section = lax.axis_index("pipe")
    lane = lax.axis_index("tensor")
    replica = lax.axis_index("dp")
    after = lax.rem(section + 1, sections)
    before = lax.rem(section + sections - 1, sections)
    mirror = sections - 1 - section
    length = fwd.shape[1]
    width = GROUP * HEAD_DIM
    columns = fwd.shape[2]
    groups = columns // width
    rows = parked_hbm.shape[2]
    heads = columns // HEAD_DIM

    def head_span(h):
        return pl.ds(pl.multiple_of(h * HEAD_DIM, HEAD_DIM), HEAD_DIM)

    def load_fwd(h):
        cols = head_span(h)
        return pltpu.make_async_copy(fwd_hbm.at[:, 0, :, cols], fwd.at[:, :, cols], fwd_sem.at[h])

    seg_copy = pltpu.make_async_copy(fwd_seg_hbm, fwd_seg, small_sem.at[0])
    tok_copy = pltpu.make_async_copy(tokens_hbm, tokens, small_sem.at[1])
    seg_copy.start()
    load_fwd(0).start()

    barrier = pltpu.get_barrier_semaphore()
    greeted = 0
    for step in range(1, tensors):
        pl.semaphore_signal(barrier, inc=1, device_id={"tensor": lax.rem(lane + step, tensors)}, device_id_type=MESH)
        greeted += 1
    for other in range(replicas):
        pl.semaphore_signal(barrier, inc=1, device_id={"pipe": mirror, "dp": other}, device_id_type=MESH)
        greeted += 1
    if sections > 2:
        for other in (after, before):
            pl.semaphore_signal(barrier, inc=1, device_id={"pipe": other}, device_id_type=MESH)
            greeted += 1

    def span(g):
        return pl.ds(pl.multiple_of(g * width, width), width)

    def load_up(g):
        return pltpu.make_async_copy(up_hbm.at[0, :, span(g)], up.at[:, span(g)], up_sem.at[g])

    def my_rows(who):
        return pl.ds(pl.multiple_of(who * rows, rows), rows)

    def parked_span(who, g):
        return pl.ds(pl.multiple_of(who * columns + g * width, width), width)

    def load_own(g):
        return pltpu.make_async_copy(
            parked_hbm.at[:, 0, :, parked_span(lane, g)], stash.at[:, my_rows(lane), span(g)], own_sem.at[g]
        )

    def send_part(step, g):
        other = lax.rem(lane + step, tensors)
        return pltpu.make_async_remote_copy(
            src_ref=parked_hbm.at[:, 0, :, parked_span(other, g)],
            dst_ref=stash.at[:, my_rows(lane), span(g)],
            send_sem=part_send.at[step - 1, g],
            recv_sem=part_recv.at[step - 1, g],
            device_id={"tensor": other},
            device_id_type=MESH,
        )

    def recv_part(step, g):
        other = lax.rem(lane + tensors - step, tensors)
        return pltpu.make_async_remote_copy(
            src_ref=parked_hbm.at[:, 0, :, parked_span(lane, g)],
            dst_ref=stash.at[:, my_rows(other), span(g)],
            send_sem=part_send.at[step - 1, g],
            recv_sem=part_recv.at[step - 1, g],
            device_id={"tensor": other},
            device_id_type=MESH,
        )

    def send_out(h):
        return pltpu.make_async_remote_copy(
            src_ref=out.at[:, head_span(h)],
            dst_ref=received_hbm.at[0, :, head_span(h)],
            send_sem=out_send.at[h],
            recv_sem=out_recv.at[h],
            device_id={"pipe": after},
            device_id_type=MESH,
        )

    def send_grads(g):
        return pltpu.make_async_remote_copy(
            src_ref=grads.at[:, :, span(g)],
            dst_ref=grads_hbm.at[:, 0, :, span(g)],
            send_sem=grad_send.at[g],
            recv_sem=grad_recv.at[g],
            device_id={"pipe": mirror},
            device_id_type=MESH,
        )

    def send_tokens(other, mine):
        return pltpu.make_async_remote_copy(
            src_ref=token_tile,
            dst_ref=token_all.at[mine],
            send_sem=tok_send.at[other],
            recv_sem=tok_recv.at[mine],
            device_id={"pipe": mirror, "dp": other},
            device_id_type=MESH,
        )

    send_segment = pltpu.make_async_remote_copy(
        src_ref=bwd_seg_hbm,
        dst_ref=bwd_seg,
        send_sem=seg_send,
        recv_sem=seg_recv,
        device_id={"pipe": mirror},
        device_id_type=MESH,
    )

    def forward(h):
        load_fwd(h).wait()
        cols = head_span(h)
        probs = softmax(fwd[0, :, cols], fwd[1, :, cols], fwd_bias[...])
        mixed = dot(probs.astype(jnp.bfloat16), fwd[2, :, cols], ((1,), (0,)))
        out[:, cols] = mixed.astype(jnp.bfloat16)

    tok_copy.start()
    pl.loop(1, heads)(lambda h: load_fwd(h).start())
    seg_copy.wait()
    fwd_bias[...] = mask_bias(fwd_seg[...])
    forward(0)
    tok_copy.wait()
    token_tile[...] = jnp.full(token_tile.shape, tokens[0], jnp.int32)

    pl.semaphore_wait(barrier, greeted)
    send_out(0).start()
    send_segment.start()
    for other in range(replicas):
        send_tokens(other, replica).start()

    def exchange(g):
        for step in range(1, tensors):
            send_part(step, g).start()

    for g in range(AHEAD):
        exchange(g)
    pl.loop(0, groups)(lambda g: load_own(g).start())
    pl.loop(0, groups)(lambda g: load_up(g).start())

    @pl.loop(1, heads)
    def _(h):
        forward(h)
        send_out(h).start()

    send_segment.wait()
    bwd_bias[...] = mask_bias(bwd_seg[...])
    total = jnp.zeros((1, HEAD_DIM), jnp.float32)
    for other in range(replicas):
        send_tokens(other, other).wait_recv()
        total += token_all[other, 0:1, :].astype(jnp.float32)
    factor = jnp.float32(replicas * length) / total

    @pl.loop(0, groups)
    def _(g):
        load_own(g).wait()
        load_up(g).wait()
        for step in range(1, tensors):
            recv_part(step, g).wait_recv()

        @pl.when(g < groups - AHEAD)
        def _():
            exchange(g + AHEAD)

        for h in range(GROUP):
            cols = pl.ds(pl.multiple_of(g * width + h * HEAD_DIM, HEAD_DIM), HEAD_DIM)
            query, key, value, upstream = stash[0, :, cols], stash[1, :, cols], stash[2, :, cols], up[:, cols]
            probs = softmax(query, key, bwd_bias[...])
            grad_value = dot(probs.astype(jnp.bfloat16), upstream, ((0,), (0,)))
            grad_probs = dot(upstream, value, ((1,), (1,)))
            center = jnp.sum(probs * grad_probs, axis=-1, keepdims=True)
            grad_logits = (probs * (grad_probs - center) * SCALE).astype(jnp.bfloat16)
            grad_query = dot(grad_logits, key, ((1,), (0,)))
            grad_key = dot(grad_logits, query, ((0,), (0,)))
            grads[0, :, cols] = (grad_query * factor).astype(jnp.bfloat16)
            grads[1, :, cols] = (grad_key * factor).astype(jnp.bfloat16)
            grads[2, :, cols] = (grad_value * factor).astype(jnp.bfloat16)
        send_grads(g).start()

    for other in range(replicas):
        send_tokens(other, replica).wait_send()

    @pl.loop(0, groups)
    def _(g):
        for step in range(1, tensors):
            send_part(step, g).wait_send()

    pl.loop(0, heads)(lambda h: send_out(h).wait())

    @pl.loop(0, groups)
    def _(g):
        send_grads(g).wait()


def store(received, grads, received_out, grads_out, sems):
    copies = [pltpu.make_async_copy(received, received_out, sems.at[0])]
    for k in range(3):
        copies.append(pltpu.make_async_copy(grads.at[k], grads_out.at[k], sems.at[1 + k]))
    for copy in copies:
        copy.start()
    for copy in copies:
        copy.wait()


def on_device(fwd_qkv, fwd_segments, parked, bwd_segments, grad_out, loss_tokens):
    sections = lax.axis_size("pipe")
    tensors = lax.axis_size("tensor")
    replicas = lax.axis_size("dp")
    length, columns = fwd_qkv.shape[2], fwd_qkv.shape[3]
    heads = columns // HEAD_DIM
    groups = heads // GROUP
    if sections > 2:
        grad_out = lax.ppermute(grad_out, "pipe", [(i, (-i) % sections) for i in range(sections)])
    dma = pltpu.SemaphoreType.DMA
    received, grads = pl.pallas_call(
        functools.partial(kernel, sections, tensors, replicas),
        out_shape=(
            jax.ShapeDtypeStruct((1, length, columns), jnp.bfloat16),
            jax.ShapeDtypeStruct((3, 1, length, columns), jnp.bfloat16),
        ),
        in_specs=[pl.BlockSpec(memory_space=pltpu.HBM)] * 6,
        out_specs=(pl.BlockSpec(memory_space=pl.ANY), pl.BlockSpec(memory_space=pl.ANY)),
        scratch_shapes=[
            pltpu.VMEM((3, length, columns), jnp.bfloat16),
            pltpu.VMEM((length, columns), jnp.bfloat16),
            pltpu.VMEM((3, length, columns), jnp.bfloat16),
            pltpu.VMEM((length, columns), jnp.bfloat16),
            pltpu.VMEM((3, length, columns), jnp.bfloat16),
            pltpu.VMEM((length, length), jnp.float32),
            pltpu.VMEM((length, length), jnp.float32),
            pltpu.VMEM((1, length), jnp.int32),
            pltpu.VMEM((1, length), jnp.int32),
            pltpu.SMEM((1,), jnp.int32),
            pltpu.VMEM((8, HEAD_DIM), jnp.int32),
            pltpu.VMEM((replicas, 8, HEAD_DIM), jnp.int32),
            dma((heads,)), dma((groups,)), dma((groups,)), dma((2,)),
            dma((tensors - 1, groups)), dma((tensors - 1, groups)),
            dma((heads,)), dma((heads,)), dma((groups,)), dma((groups,)),
            dma, dma, dma((replicas,)), dma((replicas,)),
        ],
        compiler_params=pltpu.CompilerParams(
            collective_id=0, has_side_effects=True, vmem_limit_bytes=48 * 1024 * 1024
        ),
        cost_estimate=pl.CostEstimate(
            flops=14 * length * length * columns, bytes_accessed=22 * length * columns, transcendentals=0
        ),
    )(*(pltpu.with_memory_space_constraint(x, pltpu.HBM) for x in (fwd_qkv, fwd_segments, parked, bwd_segments, grad_out)), loss_tokens)
    return pl.pallas_call(
        store,
        out_shape=(
            jax.ShapeDtypeStruct(received.shape, jnp.bfloat16),
            jax.ShapeDtypeStruct(grads.shape, jnp.bfloat16),
        ),
        in_specs=[pl.BlockSpec(memory_space=pl.ANY)] * 2,
        out_specs=(pl.BlockSpec(memory_space=pl.ANY), pl.BlockSpec(memory_space=pl.ANY)),
        scratch_shapes=[dma((4,))],
        compiler_params=pltpu.CompilerParams(vmem_limit_bytes=1024 * 1024),
    )(received, grads)


def solution(mesh):
    placed = (
        P(None, ("pipe", "dp"), None, "tensor"),
        P(("pipe", "dp"), None),
        P(None, ("pipe", "dp"), "tensor", None),
        P(("pipe", "dp"), None),
        P(("pipe", "dp"), None, "tensor"),
        P(("pipe", "dp")),
    )
    return jax.shard_map(
        on_device,
        mesh=mesh,
        in_specs=placed,
        out_specs=(P(("pipe", "dp"), None, "tensor"), P(None, ("pipe", "dp"), None, "tensor")),
        check_vma=False,
    )
```

```python
import functools

import jax
import jax.numpy as jnp
from jax import lax
from jax.experimental import pallas as pl
from jax.experimental.pallas import tpu as pltpu
from jax.sharding import PartitionSpec as P

HEAD_DIM = 128
SCALE = HEAD_DIM ** (-0.5)
GROUP = 2
AHEAD = 2
MESH = pl.DeviceIdType.MESH


def dot(a, b, contract):
    return lax.dot_general(a, b, (contract, ((), ())), preferred_element_type=jnp.float32)


def softmax(query, key, bias):
    logits = dot(query, key, ((1,), (1,))) * SCALE + bias
    weights = jnp.exp(logits - jnp.max(logits, axis=-1, keepdims=True))
    return weights / jnp.sum(weights, axis=-1, keepdims=True)


def mask_bias(segment):
    length = segment.shape[1]
    along = jnp.broadcast_to(segment.astype(jnp.float32), (length, length))
    return jnp.where(along == along.T, jnp.float32(0), jnp.float32(-1e30))


def kernel(
    sections, tensors, replicas,
    fwd_hbm, fwd_seg_hbm, parked_hbm, bwd_seg_hbm, up_hbm, tokens_hbm,
    landed_out, landed_grads,
    fwd, out, stash, up, grads, fwd_bias, bwd_bias, fwd_seg, bwd_seg, tokens, token_tile, token_all,
    fwd_sem, up_sem, own_sem, small_sem,
    part_send, part_recv, out_send, out_recv, grad_send, grad_recv,
    seg_send, seg_recv, tok_send, tok_recv,
):
    section = lax.axis_index("pipe")
    lane = lax.axis_index("tensor")
    replica = lax.axis_index("dp")
    after = lax.rem(section + 1, sections)
    before = lax.rem(section + sections - 1, sections)
    mirror = sections - 1 - section
    length = fwd.shape[1]
    width = GROUP * HEAD_DIM
    columns = fwd.shape[2]
    groups = columns // width
    rows = parked_hbm.shape[2]
    heads = columns // HEAD_DIM

    def head_span(h):
        return pl.ds(pl.multiple_of(h * HEAD_DIM, HEAD_DIM), HEAD_DIM)

    def load_fwd(h):
        cols = head_span(h)
        return pltpu.make_async_copy(fwd_hbm.at[:, 0, :, cols], fwd.at[:, :, cols], fwd_sem.at[h])

    seg_copy = pltpu.make_async_copy(fwd_seg_hbm, fwd_seg, small_sem.at[0])
    tok_copy = pltpu.make_async_copy(tokens_hbm, tokens, small_sem.at[1])
    seg_copy.start()
    load_fwd(0).start()

    barrier = pltpu.get_barrier_semaphore()
    greeted = 0
    for step in range(1, tensors):
        pl.semaphore_signal(barrier, inc=1, device_id={"tensor": lax.rem(lane + step, tensors)}, device_id_type=MESH)
        greeted += 1
    for other in range(replicas):
        pl.semaphore_signal(barrier, inc=1, device_id={"pipe": mirror, "dp": other}, device_id_type=MESH)
        greeted += 1
    if sections > 2:
        for other in (after, before):
            pl.semaphore_signal(barrier, inc=1, device_id={"pipe": other}, device_id_type=MESH)
            greeted += 1

    def span(g):
        return pl.ds(pl.multiple_of(g * width, width), width)

    def load_up(g):
        return pltpu.make_async_copy(up_hbm.at[0, :, span(g)], up.at[:, span(g)], up_sem.at[g])

    def my_rows(who):
        return pl.ds(pl.multiple_of(who * rows, rows), rows)

    def parked_span(who, g):
        return pl.ds(pl.multiple_of(who * columns + g * width, width), width)

    def load_own(g):
        return pltpu.make_async_copy(
            parked_hbm.at[:, 0, :, parked_span(lane, g)], stash.at[:, my_rows(lane), span(g)], own_sem.at[g]
        )

    def send_part(step, g):
        other = lax.rem(lane + step, tensors)
        return pltpu.make_async_remote_copy(
            src_ref=parked_hbm.at[:, 0, :, parked_span(other, g)],
            dst_ref=stash.at[:, my_rows(lane), span(g)],
            send_sem=part_send.at[step - 1, g],
            recv_sem=part_recv.at[step - 1, g],
            device_id={"tensor": other},
            device_id_type=MESH,
        )

    def recv_part(step, g):
        other = lax.rem(lane + tensors - step, tensors)
        return pltpu.make_async_remote_copy(
            src_ref=parked_hbm.at[:, 0, :, parked_span(lane, g)],
            dst_ref=stash.at[:, my_rows(other), span(g)],
            send_sem=part_send.at[step - 1, g],
            recv_sem=part_recv.at[step - 1, g],
            device_id={"tensor": other},
            device_id_type=MESH,
        )

    def send_out(h):
        return pltpu.make_async_remote_copy(
            src_ref=out.at[h],
            dst_ref=landed_out.at[h],
            send_sem=out_send.at[h],
            recv_sem=out_recv.at[h],
            device_id={"pipe": after},
            device_id_type=MESH,
        )

    def send_grads(g):
        return pltpu.make_async_remote_copy(
            src_ref=grads.at[g],
            dst_ref=landed_grads.at[g],
            send_sem=grad_send.at[g],
            recv_sem=grad_recv.at[g],
            device_id={"pipe": mirror},
            device_id_type=MESH,
        )

    def send_tokens(other, mine):
        return pltpu.make_async_remote_copy(
            src_ref=token_tile,
            dst_ref=token_all.at[mine],
            send_sem=tok_send.at[other],
            recv_sem=tok_recv.at[mine],
            device_id={"pipe": mirror, "dp": other},
            device_id_type=MESH,
        )

    send_segment = pltpu.make_async_remote_copy(
        src_ref=bwd_seg_hbm,
        dst_ref=bwd_seg,
        send_sem=seg_send,
        recv_sem=seg_recv,
        device_id={"pipe": mirror},
        device_id_type=MESH,
    )

    def forward(h):
        load_fwd(h).wait()
        cols = head_span(h)
        probs = softmax(fwd[0, :, cols], fwd[1, :, cols], fwd_bias[...])
        mixed = dot(probs.astype(jnp.bfloat16), fwd[2, :, cols], ((1,), (0,)))
        out[h] = mixed.astype(jnp.bfloat16)

    tok_copy.start()
    pl.loop(1, heads)(lambda h: load_fwd(h).start())
    seg_copy.wait()
    fwd_bias[...] = mask_bias(fwd_seg[...])
    forward(0)
    tok_copy.wait()
    token_tile[...] = jnp.full(token_tile.shape, tokens[0], jnp.int32)

    pl.semaphore_wait(barrier, greeted)
    send_out(0).start()
    send_segment.start()
    for other in range(replicas):
        send_tokens(other, replica).start()

    def exchange(g):
        for step in range(1, tensors):
            send_part(step, g).start()

    for g in range(AHEAD):
        exchange(g)
    pl.loop(0, groups)(lambda g: load_own(g).start())
    pl.loop(0, groups)(lambda g: load_up(g).start())

    @pl.loop(1, heads)
    def _(h):
        forward(h)
        send_out(h).start()

    send_segment.wait()
    bwd_bias[...] = mask_bias(bwd_seg[...])
    total = jnp.zeros((1, HEAD_DIM), jnp.float32)
    for other in range(replicas):
        send_tokens(other, other).wait_recv()
        total += token_all[other, 0:1, :].astype(jnp.float32)
    factor = jnp.float32(replicas * length) / total

    @pl.loop(0, groups)
    def _(g):
        load_own(g).wait()
        load_up(g).wait()
        for step in range(1, tensors):
            recv_part(step, g).wait_recv()

        @pl.when(g < groups - AHEAD)
        def _():
            exchange(g + AHEAD)

        for h in range(GROUP):
            cols = pl.ds(pl.multiple_of(g * width + h * HEAD_DIM, HEAD_DIM), HEAD_DIM)
            query, key, value, upstream = stash[0, :, cols], stash[1, :, cols], stash[2, :, cols], up[:, cols]
            probs = softmax(query, key, bwd_bias[...])
            grad_value = dot(probs.astype(jnp.bfloat16), upstream, ((0,), (0,)))
            grad_probs = dot(upstream, value, ((1,), (1,)))
            center = jnp.sum(probs * grad_probs, axis=-1, keepdims=True)
            grad_logits = (probs * (grad_probs - center) * SCALE).astype(jnp.bfloat16)
            grad_query = dot(grad_logits, key, ((1,), (0,)))
            grad_key = dot(grad_logits, query, ((0,), (0,)))
            place = slice(h * HEAD_DIM, (h + 1) * HEAD_DIM)
            grads[g, 0, :, place] = (grad_query * factor).astype(jnp.bfloat16)
            grads[g, 1, :, place] = (grad_key * factor).astype(jnp.bfloat16)
            grads[g, 2, :, place] = (grad_value * factor).astype(jnp.bfloat16)
        send_grads(g).start()

    for other in range(replicas):
        send_tokens(other, replica).wait_send()

    @pl.loop(0, groups)
    def _(g):
        for step in range(1, tensors):
            send_part(step, g).wait_send()

    pl.loop(0, heads)(lambda h: send_out(h).wait())

    @pl.loop(0, groups)
    def _(g):
        send_grads(g).wait()


def store(landed_out, landed_grads, received, grads, out_sem, grad_sem):
    heads, groups = landed_out.shape[0], landed_grads.shape[0]
    width = GROUP * HEAD_DIM

    def store_out(h):
        cols = pl.ds(h * HEAD_DIM, HEAD_DIM)
        return pltpu.make_async_copy(landed_out.at[h], received.at[0, :, cols], out_sem.at[h])

    def store_grads(g):
        cols = pl.ds(g * width, width)
        return pltpu.make_async_copy(landed_grads.at[g], grads.at[:, 0, :, cols], grad_sem.at[g])

    copies = [store_grads(g) for g in range(groups)] + [store_out(h) for h in range(heads)]
    for copy in copies:
        copy.start()
    for copy in copies:
        copy.wait()


def on_device(fwd_qkv, fwd_segments, parked, bwd_segments, grad_out, loss_tokens):
    sections = lax.axis_size("pipe")
    tensors = lax.axis_size("tensor")
    replicas = lax.axis_size("dp")
    length, columns = fwd_qkv.shape[2], fwd_qkv.shape[3]
    heads = columns // HEAD_DIM
    groups = heads // GROUP
    if sections > 2:
        grad_out = lax.ppermute(grad_out, "pipe", [(i, (-i) % sections) for i in range(sections)])
    dma = pltpu.SemaphoreType.DMA
    landed_out, landed_grads = pl.pallas_call(
        functools.partial(kernel, sections, tensors, replicas),
        out_shape=(
            jax.ShapeDtypeStruct((heads, length, HEAD_DIM), jnp.bfloat16),
            jax.ShapeDtypeStruct((groups, 3, length, GROUP * HEAD_DIM), jnp.bfloat16),
        ),
        in_specs=[pl.BlockSpec(memory_space=pltpu.HBM)] * 6,
        out_specs=(pl.BlockSpec(memory_space=pl.ANY), pl.BlockSpec(memory_space=pl.ANY)),
        scratch_shapes=[
            pltpu.VMEM((3, length, columns), jnp.bfloat16),
            pltpu.VMEM((heads, length, HEAD_DIM), jnp.bfloat16),
            pltpu.VMEM((3, length, columns), jnp.bfloat16),
            pltpu.VMEM((length, columns), jnp.bfloat16),
            pltpu.VMEM((groups, 3, length, GROUP * HEAD_DIM), jnp.bfloat16),
            pltpu.VMEM((length, length), jnp.float32),
            pltpu.VMEM((length, length), jnp.float32),
            pltpu.VMEM((1, length), jnp.int32),
            pltpu.VMEM((1, length), jnp.int32),
            pltpu.SMEM((1,), jnp.int32),
            pltpu.VMEM((8, HEAD_DIM), jnp.int32),
            pltpu.VMEM((replicas, 8, HEAD_DIM), jnp.int32),
            dma((heads,)), dma((groups,)), dma((groups,)), dma((2,)),
            dma((tensors - 1, groups)), dma((tensors - 1, groups)),
            dma((heads,)), dma((heads,)), dma((groups,)), dma((groups,)),
            dma, dma, dma((replicas,)), dma((replicas,)),
        ],
        compiler_params=pltpu.CompilerParams(
            collective_id=0, has_side_effects=True, vmem_limit_bytes=48 * 1024 * 1024
        ),
        cost_estimate=pl.CostEstimate(
            flops=14 * length * length * columns, bytes_accessed=22 * length * columns, transcendentals=0
        ),
    )(*(pltpu.with_memory_space_constraint(x, pltpu.HBM) for x in (fwd_qkv, fwd_segments, parked, bwd_segments, grad_out)), loss_tokens)
    return pl.pallas_call(
        store,
        out_shape=(
            jax.ShapeDtypeStruct((1, length, columns), jnp.bfloat16),
            jax.ShapeDtypeStruct((3, 1, length, columns), jnp.bfloat16),
        ),
        in_specs=[pl.BlockSpec(memory_space=pl.ANY)] * 2,
        out_specs=(pl.BlockSpec(memory_space=pl.ANY), pl.BlockSpec(memory_space=pl.ANY)),
        scratch_shapes=[dma((heads,)), dma((groups,))],
        compiler_params=pltpu.CompilerParams(vmem_limit_bytes=1024 * 1024),
    )(landed_out, landed_grads)


def solution(mesh):
    placed = (
        P(None, ("pipe", "dp"), None, "tensor"),
        P(("pipe", "dp"), None),
        P(None, ("pipe", "dp"), "tensor", None),
        P(("pipe", "dp"), None),
        P(("pipe", "dp"), None, "tensor"),
        P(("pipe", "dp")),
    )
    return jax.shard_map(
        on_device,
        mesh=mesh,
        in_specs=placed,
        out_specs=(P(("pipe", "dp"), None, "tensor"), P(None, ("pipe", "dp"), None, "tensor")),
        check_vma=False,
    )
```

```python
import functools

import jax
import jax.numpy as jnp
from jax import lax
from jax.experimental import pallas as pl
from jax.experimental.pallas import tpu as pltpu
from jax.sharding import PartitionSpec as P

HEAD_DIM = 128
SCALE = HEAD_DIM ** (-0.5)
GROUP = 2
AHEAD = 2
SPREAD_AT, TOTAL_AT = 2, 6
MESH = pl.DeviceIdType.MESH


def dot(a, b, contract):
    return lax.dot_general(a, b, (contract, ((), ())), preferred_element_type=jnp.float32)


def softmax(query, key, bias):
    logits = dot(query, key, ((1,), (1,))) * SCALE + bias
    weights = jnp.exp(logits - jnp.max(logits, axis=-1, keepdims=True))
    return weights / jnp.sum(weights, axis=-1, keepdims=True)


def mask_bias(segment):
    length = segment.shape[1]
    along = jnp.broadcast_to(segment.astype(jnp.float32), (length, length))
    return jnp.where(along == along.T, jnp.float32(0), jnp.float32(-1e30))


def kernel(
    sections, tensors, replicas,
    fwd_hbm, fwd_seg_hbm, parked_hbm, bwd_seg_hbm, up_hbm, tokens_hbm,
    received_hbm, grads_hbm,
    fwd, out, stash, up, grads, fwd_bias, bwd_bias, fwd_seg, bwd_seg, tokens,
    token_tile, token_got, token_all, token_total,
    fwd_sem, up_sem, own_sem, small_sem,
    part_send, part_recv, out_send, out_recv, grad_send, grad_recv,
    seg_send, seg_recv, tok_send, tok_recv, spread_send, spread_recv, total_send, total_recv,
):
    section = lax.axis_index("pipe")
    lane = lax.axis_index("tensor")
    replica = lax.axis_index("dp")
    after = lax.rem(section + 1, sections)
    before = lax.rem(section + sections - 1, sections)
    mirror = sections - 1 - section
    length = fwd.shape[1]
    width = GROUP * HEAD_DIM
    columns = fwd.shape[2]
    groups = columns // width
    rows = parked_hbm.shape[2]
    heads = columns // HEAD_DIM

    def head_span(h):
        return pl.ds(pl.multiple_of(h * HEAD_DIM, HEAD_DIM), HEAD_DIM)

    def load_fwd(h):
        cols = head_span(h)
        return pltpu.make_async_copy(fwd_hbm.at[:, 0, :, cols], fwd.at[:, :, cols], fwd_sem.at[h])

    seg_copy = pltpu.make_async_copy(fwd_seg_hbm, fwd_seg, small_sem.at[0])
    tok_copy = pltpu.make_async_copy(tokens_hbm, tokens, small_sem.at[1])
    seg_copy.start()
    load_fwd(0).start()

    barrier = pltpu.get_barrier_semaphore()
    greeted = 0
    for step in range(1, tensors):
        pl.semaphore_signal(barrier, inc=1, device_id={"tensor": lax.rem(lane + step, tensors)}, device_id_type=MESH)
        greeted += 1
    pl.semaphore_signal(barrier, inc=1, device_id={"pipe": mirror}, device_id_type=MESH)
    greeted += 1
    if sections > 2:
        for other in (after, before):
            pl.semaphore_signal(barrier, inc=1, device_id={"pipe": other}, device_id_type=MESH)
            greeted += 1

    relays = lane == tensors - 1

    def other_replica(step):
        return lax.rem(replica + step, replicas)

    @pl.when(relays)
    def _():
        for step in range(1, replicas):
            pl.semaphore_signal(barrier, inc=1, device_id={"dp": other_replica(step)}, device_id_type=MESH)

    def span(g):
        return pl.ds(pl.multiple_of(g * width, width), width)

    def load_up(g):
        return pltpu.make_async_copy(up_hbm.at[0, :, span(g)], up.at[:, span(g)], up_sem.at[g])

    def my_rows(who):
        return pl.ds(pl.multiple_of(who * rows, rows), rows)

    def parked_span(who, g):
        return pl.ds(pl.multiple_of(who * columns + g * width, width), width)

    def load_own(g):
        return pltpu.make_async_copy(
            parked_hbm.at[:, 0, :, parked_span(lane, g)], stash.at[:, my_rows(lane), span(g)], own_sem.at[g]
        )

    def send_part(step, g):
        other = lax.rem(lane + step, tensors)
        return pltpu.make_async_remote_copy(
            src_ref=parked_hbm.at[:, 0, :, parked_span(other, g)],
            dst_ref=stash.at[:, my_rows(lane), span(g)],
            send_sem=part_send.at[step - 1, g],
            recv_sem=part_recv.at[step - 1, g],
            device_id={"tensor": other},
            device_id_type=MESH,
        )

    def recv_part(step, g):
        other = lax.rem(lane + tensors - step, tensors)
        return pltpu.make_async_remote_copy(
            src_ref=parked_hbm.at[:, 0, :, parked_span(lane, g)],
            dst_ref=stash.at[:, my_rows(other), span(g)],
            send_sem=part_send.at[step - 1, g],
            recv_sem=part_recv.at[step - 1, g],
            device_id={"tensor": other},
            device_id_type=MESH,
        )

    def send_out(h):
        return pltpu.make_async_remote_copy(
            src_ref=out.at[:, head_span(h)],
            dst_ref=received_hbm.at[0, :, head_span(h)],
            send_sem=out_send.at[h],
            recv_sem=out_recv.at[h],
            device_id={"pipe": after},
            device_id_type=MESH,
        )

    def send_grads(g):
        return pltpu.make_async_remote_copy(
            src_ref=grads.at[:, :, span(g)],
            dst_ref=grads_hbm.at[:, 0, :, span(g)],
            send_sem=grad_send.at[g],
            recv_sem=grad_recv.at[g],
            device_id={"pipe": mirror},
            device_id_type=MESH,
        )

    send_tokens = pltpu.make_async_remote_copy(
        src_ref=token_tile,
        dst_ref=token_got,
        send_sem=tok_send,
        recv_sem=tok_recv,
        device_id={"pipe": mirror},
        device_id_type=MESH,
    )

    def spread_tokens(step):
        return pltpu.make_async_remote_copy(
            src_ref=token_got,
            dst_ref=token_all.at[step - 1],
            send_sem=spread_send.at[step - 1],
            recv_sem=spread_recv.at[step - 1],
            device_id={"dp": other_replica(step)},
            device_id_type=MESH,
        )

    def hand_total(step):
        return pltpu.make_async_remote_copy(
            src_ref=token_total,
            dst_ref=token_total,
            send_sem=total_send.at[step - 1],
            recv_sem=total_recv,
            device_id={"tensor": lax.rem(lane + step, tensors)},
            device_id_type=MESH,
        )

    send_segment = pltpu.make_async_remote_copy(
        src_ref=bwd_seg_hbm,
        dst_ref=bwd_seg,
        send_sem=seg_send,
        recv_sem=seg_recv,
        device_id={"pipe": mirror},
        device_id_type=MESH,
    )

    def forward(h):
        load_fwd(h).wait()
        cols = head_span(h)
        probs = softmax(fwd[0, :, cols], fwd[1, :, cols], fwd_bias[...])
        mixed = dot(probs.astype(jnp.bfloat16), fwd[2, :, cols], ((1,), (0,)))
        out[:, cols] = mixed.astype(jnp.bfloat16)

    tok_copy.start()
    pl.loop(1, heads)(lambda h: load_fwd(h).start())
    seg_copy.wait()
    fwd_bias[...] = mask_bias(fwd_seg[...])
    forward(0)
    tok_copy.wait()
    token_tile[...] = jnp.full(token_tile.shape, tokens[0], jnp.int32)

    @pl.when(relays)
    def _():
        pl.semaphore_wait(barrier, greeted + replicas - 1)
        send_tokens.start()

    @pl.when(lane != tensors - 1)
    def _():
        pl.semaphore_wait(barrier, greeted)

    send_segment.start()
    send_out(0).start()

    def exchange(g):
        for step in range(1, tensors):
            send_part(step, g).start()

    for g in range(AHEAD):
        exchange(g)
    pl.loop(0, groups)(lambda g: load_own(g).start())
    pl.loop(0, groups)(lambda g: load_up(g).start())

    @pl.loop(1, heads)
    def _(h):
        forward(h)
        send_out(h).start()

        @pl.when(relays & (h == SPREAD_AT))
        def _():
            send_tokens.wait()
            for step in range(1, replicas):
                spread_tokens(step).start()

        @pl.when(relays & (h == TOTAL_AT))
        def _():
            total = token_got[...]
            for step in range(1, replicas):
                spread_tokens(step).wait()
                total += token_all[step - 1]
            token_total[...] = total
            for step in range(1, tensors):
                hand_total(step).start()

    send_segment.wait()
    bwd_bias[...] = mask_bias(bwd_seg[...])

    @pl.when(lane != tensors - 1)
    def _():
        hand_total(1).wait_recv()

    factor = jnp.float32(replicas * length) / token_total[0:1, :].astype(jnp.float32)

    @pl.loop(0, groups)
    def _(g):
        load_own(g).wait()
        load_up(g).wait()
        for step in range(1, tensors):
            recv_part(step, g).wait_recv()

        @pl.when(g < groups - AHEAD)
        def _():
            exchange(g + AHEAD)

        for h in range(GROUP):
            cols = pl.ds(pl.multiple_of(g * width + h * HEAD_DIM, HEAD_DIM), HEAD_DIM)
            query, key, value, upstream = stash[0, :, cols], stash[1, :, cols], stash[2, :, cols], up[:, cols]
            probs = softmax(query, key, bwd_bias[...])
            grad_value = dot(probs.astype(jnp.bfloat16), upstream, ((0,), (0,)))
            grad_probs = dot(upstream, value, ((1,), (1,)))
            center = jnp.sum(probs * grad_probs, axis=-1, keepdims=True)
            grad_logits = (probs * (grad_probs - center) * SCALE).astype(jnp.bfloat16)
            grad_query = dot(grad_logits, key, ((1,), (0,)))
            grad_key = dot(grad_logits, query, ((0,), (0,)))
            grads[0, :, cols] = (grad_query * factor).astype(jnp.bfloat16)
            grads[1, :, cols] = (grad_key * factor).astype(jnp.bfloat16)
            grads[2, :, cols] = (grad_value * factor).astype(jnp.bfloat16)
        send_grads(g).start()

    @pl.when(relays)
    def _():
        for step in range(1, tensors):
            hand_total(step).wait_send()

    @pl.loop(0, groups)
    def _(g):
        for step in range(1, tensors):
            send_part(step, g).wait_send()

    pl.loop(0, heads)(lambda h: send_out(h).wait())

    @pl.loop(0, groups)
    def _(g):
        send_grads(g).wait()


def store(received, grads, received_out, grads_out, sems):
    copies = [pltpu.make_async_copy(received, received_out, sems.at[0])]
    for k in range(3):
        copies.append(pltpu.make_async_copy(grads.at[k], grads_out.at[k], sems.at[1 + k]))
    for copy in copies:
        copy.start()
    for copy in copies:
        copy.wait()


def on_device(fwd_qkv, fwd_segments, parked, bwd_segments, grad_out, loss_tokens):
    sections = lax.axis_size("pipe")
    tensors = lax.axis_size("tensor")
    replicas = lax.axis_size("dp")
    length, columns = fwd_qkv.shape[2], fwd_qkv.shape[3]
    heads = columns // HEAD_DIM
    groups = heads // GROUP
    if sections > 2:
        grad_out = lax.ppermute(grad_out, "pipe", [(i, (-i) % sections) for i in range(sections)])
    dma = pltpu.SemaphoreType.DMA
    received, grads = pl.pallas_call(
        functools.partial(kernel, sections, tensors, replicas),
        out_shape=(
            jax.ShapeDtypeStruct((1, length, columns), jnp.bfloat16),
            jax.ShapeDtypeStruct((3, 1, length, columns), jnp.bfloat16),
        ),
        in_specs=[pl.BlockSpec(memory_space=pltpu.HBM)] * 6,
        out_specs=(pl.BlockSpec(memory_space=pl.ANY), pl.BlockSpec(memory_space=pl.ANY)),
        scratch_shapes=[
            pltpu.VMEM((3, length, columns), jnp.bfloat16),
            pltpu.VMEM((length, columns), jnp.bfloat16),
            pltpu.VMEM((3, length, columns), jnp.bfloat16),
            pltpu.VMEM((length, columns), jnp.bfloat16),
            pltpu.VMEM((3, length, columns), jnp.bfloat16),
            pltpu.VMEM((length, length), jnp.float32),
            pltpu.VMEM((length, length), jnp.float32),
            pltpu.VMEM((1, length), jnp.int32),
            pltpu.VMEM((1, length), jnp.int32),
            pltpu.SMEM((1,), jnp.int32),
            pltpu.VMEM((8, HEAD_DIM), jnp.int32),
            pltpu.VMEM((8, HEAD_DIM), jnp.int32),
            pltpu.VMEM((replicas - 1, 8, HEAD_DIM), jnp.int32),
            pltpu.VMEM((8, HEAD_DIM), jnp.int32),
            dma((heads,)), dma((groups,)), dma((groups,)), dma((2,)),
            dma((tensors - 1, groups)), dma((tensors - 1, groups)),
            dma((heads,)), dma((heads,)), dma((groups,)), dma((groups,)),
            dma, dma, dma, dma, dma((replicas - 1,)), dma((replicas - 1,)), dma((tensors - 1,)), dma,
        ],
        compiler_params=pltpu.CompilerParams(
            collective_id=0, has_side_effects=True, vmem_limit_bytes=48 * 1024 * 1024
        ),
        cost_estimate=pl.CostEstimate(
            flops=14 * length * length * columns, bytes_accessed=22 * length * columns, transcendentals=0
        ),
    )(*(pltpu.with_memory_space_constraint(x, pltpu.HBM) for x in (fwd_qkv, fwd_segments, parked, bwd_segments, grad_out)), loss_tokens)
    return pl.pallas_call(
        store,
        out_shape=(
            jax.ShapeDtypeStruct(received.shape, jnp.bfloat16),
            jax.ShapeDtypeStruct(grads.shape, jnp.bfloat16),
        ),
        in_specs=[pl.BlockSpec(memory_space=pl.ANY)] * 2,
        out_specs=(pl.BlockSpec(memory_space=pl.ANY), pl.BlockSpec(memory_space=pl.ANY)),
        scratch_shapes=[dma((4,))],
        compiler_params=pltpu.CompilerParams(vmem_limit_bytes=1024 * 1024),
    )(received, grads)


def solution(mesh):
    placed = (
        P(None, ("pipe", "dp"), None, "tensor"),
        P(("pipe", "dp"), None),
        P(None, ("pipe", "dp"), "tensor", None),
        P(("pipe", "dp"), None),
        P(("pipe", "dp"), None, "tensor"),
        P(("pipe", "dp")),
    )
    return jax.shard_map(
        on_device,
        mesh=mesh,
        in_specs=placed,
        out_specs=(P(("pipe", "dp"), None, "tensor"), P(None, ("pipe", "dp"), None, "tensor")),
        check_vma=False,
    )
```

```python
import functools

import jax
import jax.numpy as jnp
from jax import lax
from jax.experimental import pallas as pl
from jax.experimental.pallas import tpu as pltpu
from jax.sharding import PartitionSpec as P

HEAD_DIM = 128
SCALE = HEAD_DIM ** (-0.5)
GROUP = 2
AHEAD = 2
SPREAD_AT, TOTAL_AT = 2, 5
FIRST = 6
MESH = pl.DeviceIdType.MESH


def dot(a, b, contract):
    return lax.dot_general(a, b, (contract, ((), ())), preferred_element_type=jnp.float32)


def softmax(query, key, bias):
    logits = dot(query, key, ((1,), (1,))) * SCALE + bias
    weights = jnp.exp(logits - jnp.max(logits, axis=-1, keepdims=True))
    return weights * (1.0 / jnp.sum(weights, axis=-1, keepdims=True))


def mask_bias(segment):
    length = segment.shape[1]
    along = jnp.broadcast_to(segment.astype(jnp.float32), (length, length))
    return jnp.where(along == along.T, jnp.float32(0), jnp.float32(-1e30))


def kernel(
    sections, tensors, replicas,
    fwd_hbm, fwd_seg_hbm, parked_hbm, bwd_seg_hbm, up_hbm, tokens_hbm,
    received_hbm, grads_hbm,
    fwd, out, stash, up, grads, fwd_bias, bwd_bias, fwd_seg, bwd_seg, tokens,
    token_tile, token_got, token_all, token_total,
    fwd_sem, up_sem, own_sem, small_sem,
    part_send, part_recv, out_send, out_recv, grad_send, grad_recv,
    seg_send, seg_recv, tok_send, tok_recv, spread_send, spread_recv, total_send, total_recv,
):
    section = lax.axis_index("pipe")
    lane = lax.axis_index("tensor")
    replica = lax.axis_index("dp")
    after = lax.rem(section + 1, sections)
    before = lax.rem(section + sections - 1, sections)
    mirror = sections - 1 - section
    length = fwd.shape[1]
    width = GROUP * HEAD_DIM
    columns = fwd.shape[2]
    groups = columns // width
    rows = parked_hbm.shape[2]
    heads = columns // HEAD_DIM

    def head_span(h):
        return pl.ds(pl.multiple_of(h * HEAD_DIM, HEAD_DIM), HEAD_DIM)

    def load_fwd(h):
        cols = head_span(h)
        return pltpu.make_async_copy(fwd_hbm.at[:, 0, :, cols], fwd.at[:, :, cols], fwd_sem.at[h])

    seg_copy = pltpu.make_async_copy(fwd_seg_hbm, fwd_seg, small_sem.at[0])
    tok_copy = pltpu.make_async_copy(tokens_hbm, tokens, small_sem.at[1])
    seg_copy.start()
    load_fwd(0).start()

    barrier = pltpu.get_barrier_semaphore()
    greeted = 0
    for step in range(1, tensors):
        pl.semaphore_signal(barrier, inc=1, device_id={"tensor": lax.rem(lane + step, tensors)}, device_id_type=MESH)
        greeted += 1
    pl.semaphore_signal(barrier, inc=1, device_id={"pipe": mirror}, device_id_type=MESH)
    greeted += 1
    if sections > 2:
        for other in (after, before):
            pl.semaphore_signal(barrier, inc=1, device_id={"pipe": other}, device_id_type=MESH)
            greeted += 1

    relays = lane == tensors - 1

    def other_replica(step):
        return lax.rem(replica + step, replicas)

    @pl.when(relays)
    def _():
        for step in range(1, replicas):
            pl.semaphore_signal(barrier, inc=1, device_id={"dp": other_replica(step)}, device_id_type=MESH)

    def span(g):
        return pl.ds(pl.multiple_of(g * width, width), width)

    def load_up(g):
        return pltpu.make_async_copy(up_hbm.at[0, :, span(g)], up.at[:, span(g)], up_sem.at[g])

    def my_rows(who):
        return pl.ds(pl.multiple_of(who * rows, rows), rows)

    def parked_span(who, g):
        return pl.ds(pl.multiple_of(who * columns + g * width, width), width)

    def load_own(g):
        return pltpu.make_async_copy(
            parked_hbm.at[:, 0, :, parked_span(lane, g)], stash.at[:, my_rows(lane), span(g)], own_sem.at[g]
        )

    def send_part(step, g):
        other = lax.rem(lane + step, tensors)
        return pltpu.make_async_remote_copy(
            src_ref=parked_hbm.at[:, 0, :, parked_span(other, g)],
            dst_ref=stash.at[:, my_rows(lane), span(g)],
            send_sem=part_send.at[step - 1, g],
            recv_sem=part_recv.at[step - 1, g],
            device_id={"tensor": other},
            device_id_type=MESH,
        )

    def recv_part(step, g):
        other = lax.rem(lane + tensors - step, tensors)
        return pltpu.make_async_remote_copy(
            src_ref=parked_hbm.at[:, 0, :, parked_span(lane, g)],
            dst_ref=stash.at[:, my_rows(other), span(g)],
            send_sem=part_send.at[step - 1, g],
            recv_sem=part_recv.at[step - 1, g],
            device_id={"tensor": other},
            device_id_type=MESH,
        )

    def send_out(h):
        return pltpu.make_async_remote_copy(
            src_ref=out.at[:, head_span(h)],
            dst_ref=received_hbm.at[0, :, head_span(h)],
            send_sem=out_send.at[h],
            recv_sem=out_recv.at[h],
            device_id={"pipe": after},
            device_id_type=MESH,
        )

    def send_grads(g):
        return pltpu.make_async_remote_copy(
            src_ref=grads.at[:, :, span(g)],
            dst_ref=grads_hbm.at[:, 0, :, span(g)],
            send_sem=grad_send.at[g],
            recv_sem=grad_recv.at[g],
            device_id={"pipe": mirror},
            device_id_type=MESH,
        )

    send_tokens = pltpu.make_async_remote_copy(
        src_ref=token_tile,
        dst_ref=token_got,
        send_sem=tok_send,
        recv_sem=tok_recv,
        device_id={"pipe": mirror},
        device_id_type=MESH,
    )

    def spread_tokens(step):
        return pltpu.make_async_remote_copy(
            src_ref=token_got,
            dst_ref=token_all.at[step - 1],
            send_sem=spread_send.at[step - 1],
            recv_sem=spread_recv.at[step - 1],
            device_id={"dp": other_replica(step)},
            device_id_type=MESH,
        )

    def hand_total(step):
        return pltpu.make_async_remote_copy(
            src_ref=token_total,
            dst_ref=token_total,
            send_sem=total_send.at[step - 1],
            recv_sem=total_recv,
            device_id={"tensor": lax.rem(lane + step, tensors)},
            device_id_type=MESH,
        )

    send_segment = pltpu.make_async_remote_copy(
        src_ref=bwd_seg_hbm,
        dst_ref=bwd_seg,
        send_sem=seg_send,
        recv_sem=seg_recv,
        device_id={"pipe": mirror},
        device_id_type=MESH,
    )

    def forward(h):
        load_fwd(h).wait()
        cols = head_span(h)
        probs = softmax(fwd[0, :, cols], fwd[1, :, cols], fwd_bias[...])
        mixed = dot(probs.astype(jnp.bfloat16), fwd[2, :, cols], ((1,), (0,)))
        out[:, cols] = mixed.astype(jnp.bfloat16)

    tok_copy.start()
    pl.loop(1, heads)(lambda h: load_fwd(h).start())
    seg_copy.wait()
    fwd_bias[...] = mask_bias(fwd_seg[...])
    forward(0)
    tok_copy.wait()
    token_tile[...] = jnp.full(token_tile.shape, tokens[0], jnp.int32)

    @pl.when(relays)
    def _():
        pl.semaphore_wait(barrier, greeted + replicas - 1)
        send_tokens.start()

    @pl.when(lane != tensors - 1)
    def _():
        pl.semaphore_wait(barrier, greeted)

    send_segment.start()
    send_out(0).start()

    def exchange(g):
        for step in range(1, tensors):
            send_part(step, g).start()

    for g in range(AHEAD):
        exchange(g)
    pl.loop(0, groups)(lambda g: load_own(g).start())
    pl.loop(0, groups)(lambda g: load_up(g).start())

    @pl.loop(1, FIRST)
    def _(h):
        forward(h)
        send_out(h).start()

        @pl.when(relays & (h == SPREAD_AT))
        def _():
            send_tokens.wait()
            for step in range(1, replicas):
                spread_tokens(step).start()

        @pl.when(relays & (h == TOTAL_AT))
        def _():
            total = token_got[...]
            for step in range(1, replicas):
                spread_tokens(step).wait()
                total += token_all[step - 1]
            token_total[...] = total
            for step in range(1, tensors):
                hand_total(step).start()

    send_segment.wait()
    bwd_bias[...] = mask_bias(bwd_seg[...])

    @pl.when(lane != tensors - 1)
    def _():
        hand_total(1).wait_recv()

    factor = jnp.float32(replicas * length) / token_total[0:1, :].astype(jnp.float32)

    @pl.loop(0, groups)
    def _(g):
        load_own(g).wait()
        load_up(g).wait()
        for step in range(1, tensors):
            recv_part(step, g).wait_recv()

        @pl.when(g < groups - AHEAD)
        def _():
            exchange(g + AHEAD)

        for h in range(GROUP):
            cols = pl.ds(pl.multiple_of(g * width + h * HEAD_DIM, HEAD_DIM), HEAD_DIM)
            query, key, value, upstream = stash[0, :, cols], stash[1, :, cols], stash[2, :, cols], up[:, cols]
            probs = softmax(query, key, bwd_bias[...])
            grad_value = dot(probs.astype(jnp.bfloat16), upstream, ((0,), (0,)))
            grad_probs = dot(upstream, value, ((1,), (1,)))
            center = jnp.sum(probs * grad_probs, axis=-1, keepdims=True)
            grad_logits = (probs * (grad_probs - center) * SCALE).astype(jnp.bfloat16)
            grad_query = dot(grad_logits, key, ((1,), (0,)))
            grad_key = dot(grad_logits, query, ((0,), (0,)))
            grads[0, :, cols] = (grad_query * factor).astype(jnp.bfloat16)
            grads[1, :, cols] = (grad_key * factor).astype(jnp.bfloat16)
            grads[2, :, cols] = (grad_value * factor).astype(jnp.bfloat16)
        send_grads(g).start()

        @pl.when(FIRST + GROUP * g < heads)
        def _():
            for h in range(GROUP):
                forward(FIRST + GROUP * g + h)
                send_out(FIRST + GROUP * g + h).start()

    @pl.when(relays)
    def _():
        for step in range(1, tensors):
            hand_total(step).wait_send()

    @pl.loop(0, groups)
    def _(g):
        for step in range(1, tensors):
            send_part(step, g).wait_send()

    pl.loop(0, heads)(lambda h: send_out(h).wait())

    @pl.loop(0, groups)
    def _(g):
        send_grads(g).wait()


def store(received, grads, received_out, grads_out, sems):
    copies = [pltpu.make_async_copy(received, received_out, sems.at[0])]
    for k in range(3):
        copies.append(pltpu.make_async_copy(grads.at[k], grads_out.at[k], sems.at[1 + k]))
    for copy in copies:
        copy.start()
    for copy in copies:
        copy.wait()


def on_device(fwd_qkv, fwd_segments, parked, bwd_segments, grad_out, loss_tokens):
    sections = lax.axis_size("pipe")
    tensors = lax.axis_size("tensor")
    replicas = lax.axis_size("dp")
    length, columns = fwd_qkv.shape[2], fwd_qkv.shape[3]
    heads = columns // HEAD_DIM
    groups = heads // GROUP
    if sections > 2:
        grad_out = lax.ppermute(grad_out, "pipe", [(i, (-i) % sections) for i in range(sections)])
    dma = pltpu.SemaphoreType.DMA
    received, grads = pl.pallas_call(
        functools.partial(kernel, sections, tensors, replicas),
        out_shape=(
            jax.ShapeDtypeStruct((1, length, columns), jnp.bfloat16),
            jax.ShapeDtypeStruct((3, 1, length, columns), jnp.bfloat16),
        ),
        in_specs=[pl.BlockSpec(memory_space=pltpu.HBM)] * 6,
        out_specs=(pl.BlockSpec(memory_space=pl.ANY), pl.BlockSpec(memory_space=pl.ANY)),
        scratch_shapes=[
            pltpu.VMEM((3, length, columns), jnp.bfloat16),
            pltpu.VMEM((length, columns), jnp.bfloat16),
            pltpu.VMEM((3, length, columns), jnp.bfloat16),
            pltpu.VMEM((length, columns), jnp.bfloat16),
            pltpu.VMEM((3, length, columns), jnp.bfloat16),
            pltpu.VMEM((length, length), jnp.float32),
            pltpu.VMEM((length, length), jnp.float32),
            pltpu.VMEM((1, length), jnp.int32),
            pltpu.VMEM((1, length), jnp.int32),
            pltpu.SMEM((1,), jnp.int32),
            pltpu.VMEM((8, HEAD_DIM), jnp.int32),
            pltpu.VMEM((8, HEAD_DIM), jnp.int32),
            pltpu.VMEM((replicas - 1, 8, HEAD_DIM), jnp.int32),
            pltpu.VMEM((8, HEAD_DIM), jnp.int32),
            dma((heads,)), dma((groups,)), dma((groups,)), dma((2,)),
            dma((tensors - 1, groups)), dma((tensors - 1, groups)),
            dma((heads,)), dma((heads,)), dma((groups,)), dma((groups,)),
            dma, dma, dma, dma, dma((replicas - 1,)), dma((replicas - 1,)), dma((tensors - 1,)), dma,
        ],
        compiler_params=pltpu.CompilerParams(
            collective_id=0, has_side_effects=True, vmem_limit_bytes=48 * 1024 * 1024
        ),
        cost_estimate=pl.CostEstimate(
            flops=14 * length * length * columns, bytes_accessed=22 * length * columns, transcendentals=0
        ),
    )(*(pltpu.with_memory_space_constraint(x, pltpu.HBM) for x in (fwd_qkv, fwd_segments, parked, bwd_segments, grad_out)), loss_tokens)
    return pl.pallas_call(
        store,
        out_shape=(
            jax.ShapeDtypeStruct(received.shape, jnp.bfloat16),
            jax.ShapeDtypeStruct(grads.shape, jnp.bfloat16),
        ),
        in_specs=[pl.BlockSpec(memory_space=pl.ANY)] * 2,
        out_specs=(pl.BlockSpec(memory_space=pl.ANY), pl.BlockSpec(memory_space=pl.ANY)),
        scratch_shapes=[dma((4,))],
        compiler_params=pltpu.CompilerParams(vmem_limit_bytes=1024 * 1024),
    )(received, grads)


def solution(mesh):
    placed = (
        P(None, ("pipe", "dp"), None, "tensor"),
        P(("pipe", "dp"), None),
        P(None, ("pipe", "dp"), "tensor", None),
        P(("pipe", "dp"), None),
        P(("pipe", "dp"), None, "tensor"),
        P(("pipe", "dp")),
    )
    return jax.shard_map(
        on_device,
        mesh=mesh,
        in_specs=placed,
        out_specs=(P(("pipe", "dp"), None, "tensor"), P(None, ("pipe", "dp"), None, "tensor")),
        check_vma=False,
    )
```

```python
import functools

import jax
import jax.numpy as jnp
from jax import lax
from jax.experimental import pallas as pl
from jax.experimental.pallas import tpu as pltpu
from jax.sharding import PartitionSpec as P

HEAD_DIM = 128
SCALE = HEAD_DIM ** (-0.5)
GROUP = 2
AHEAD = 2
SPREAD_AT, TOTAL_AT = 2, 6
MESH = pl.DeviceIdType.MESH


def dot(a, b, contract):
    return lax.dot_general(a, b, (contract, ((), ())), preferred_element_type=jnp.float32)


def softmax(query, key, bias):
    logits = dot(query, key, ((1,), (1,))) * SCALE + bias
    weights = jnp.exp(logits - jnp.max(logits, axis=-1, keepdims=True))
    return weights * (1.0 / jnp.sum(weights, axis=-1, keepdims=True))


def mask_bias(segment):
    length = segment.shape[1]
    along = jnp.broadcast_to(segment.astype(jnp.float32), (length, length))
    return jnp.where(along == along.T, jnp.float32(0), jnp.float32(-1e30))


def kernel(
    sections, tensors, replicas,
    fwd_hbm, fwd_seg_hbm, parked_hbm, bwd_seg_hbm, up_hbm, tokens_hbm,
    received_hbm, grads_hbm,
    fwd, out, stash, up, grads, fwd_bias, bwd_bias, fwd_seg, bwd_seg, tokens,
    token_tile, token_got, token_all, token_total,
    fwd_sem, up_sem, own_sem, small_sem,
    part_send, part_recv, out_send, out_recv, grad_send, grad_recv,
    seg_send, seg_recv, tok_send, tok_recv, spread_send, spread_recv, total_send, total_recv,
):
    section = lax.axis_index("pipe")
    lane = lax.axis_index("tensor")
    replica = lax.axis_index("dp")
    after = lax.rem(section + 1, sections)
    before = lax.rem(section + sections - 1, sections)
    mirror = sections - 1 - section
    length = fwd.shape[1]
    width = GROUP * HEAD_DIM
    columns = fwd.shape[2]
    groups = columns // width
    rows = parked_hbm.shape[2]
    heads = columns // HEAD_DIM

    def head_span(h):
        return pl.ds(pl.multiple_of(h * HEAD_DIM, HEAD_DIM), HEAD_DIM)

    def load_fwd(h):
        cols = head_span(h)
        return pltpu.make_async_copy(fwd_hbm.at[:, 0, :, cols], fwd.at[:, :, cols], fwd_sem.at[h])

    seg_copy = pltpu.make_async_copy(fwd_seg_hbm, fwd_seg, small_sem.at[0])
    tok_copy = pltpu.make_async_copy(tokens_hbm, tokens, small_sem.at[1])
    seg_copy.start()
    load_fwd(0).start()
    tok_copy.start()
    load_fwd(1).start()

    barrier = pltpu.get_barrier_semaphore()
    greeted = 0
    for step in range(1, tensors):
        pl.semaphore_signal(barrier, inc=1, device_id={"tensor": lax.rem(lane + step, tensors)}, device_id_type=MESH)
        greeted += 1
    pl.semaphore_signal(barrier, inc=1, device_id={"pipe": mirror}, device_id_type=MESH)
    greeted += 1
    if sections > 2:
        for other in (after, before):
            pl.semaphore_signal(barrier, inc=1, device_id={"pipe": other}, device_id_type=MESH)
            greeted += 1

    relays = lane == tensors - 1

    def other_replica(step):
        return lax.rem(replica + step, replicas)

    @pl.when(relays)
    def _():
        for step in range(1, replicas):
            pl.semaphore_signal(barrier, inc=1, device_id={"dp": other_replica(step)}, device_id_type=MESH)

    def span(g):
        return pl.ds(pl.multiple_of(g * width, width), width)

    def load_up(g):
        return pltpu.make_async_copy(up_hbm.at[0, :, span(g)], up.at[:, span(g)], up_sem.at[g])

    def my_rows(who):
        return pl.ds(pl.multiple_of(who * rows, rows), rows)

    def parked_span(who, g):
        return pl.ds(pl.multiple_of(who * columns + g * width, width), width)

    def load_own(g):
        return pltpu.make_async_copy(
            parked_hbm.at[:, 0, :, parked_span(lane, g)], stash.at[:, my_rows(lane), span(g)], own_sem.at[g]
        )

    def send_part(step, g):
        other = lax.rem(lane + step, tensors)
        return pltpu.make_async_remote_copy(
            src_ref=parked_hbm.at[:, 0, :, parked_span(other, g)],
            dst_ref=stash.at[:, my_rows(lane), span(g)],
            send_sem=part_send.at[step - 1, g],
            recv_sem=part_recv.at[step - 1, g],
            device_id={"tensor": other},
            device_id_type=MESH,
        )

    def recv_part(step, g):
        other = lax.rem(lane + tensors - step, tensors)
        return pltpu.make_async_remote_copy(
            src_ref=parked_hbm.at[:, 0, :, parked_span(lane, g)],
            dst_ref=stash.at[:, my_rows(other), span(g)],
            send_sem=part_send.at[step - 1, g],
            recv_sem=part_recv.at[step - 1, g],
            device_id={"tensor": other},
            device_id_type=MESH,
        )

    def send_out(h):
        return pltpu.make_async_remote_copy(
            src_ref=out.at[:, head_span(h)],
            dst_ref=received_hbm.at[0, :, head_span(h)],
            send_sem=out_send.at[h],
            recv_sem=out_recv.at[h],
            device_id={"pipe": after},
            device_id_type=MESH,
        )

    def send_grads(g):
        return pltpu.make_async_remote_copy(
            src_ref=grads.at[:, :, span(g)],
            dst_ref=grads_hbm.at[:, 0, :, span(g)],
            send_sem=grad_send.at[g],
            recv_sem=grad_recv.at[g],
            device_id={"pipe": mirror},
            device_id_type=MESH,
        )

    def send_first(half):
        part = pl.ds(half * (length // 2), length // 2)
        place = pl.ds(0, HEAD_DIM)
        return pltpu.make_async_remote_copy(
            src_ref=out.at[part, place],
            dst_ref=received_hbm.at[0, part, place],
            send_sem=out_send.at[half * heads],
            recv_sem=out_recv.at[half * heads],
            device_id={"pipe": after},
            device_id_type=MESH,
        )

    send_tokens = pltpu.make_async_remote_copy(
        src_ref=token_tile,
        dst_ref=token_got,
        send_sem=tok_send,
        recv_sem=tok_recv,
        device_id={"pipe": mirror},
        device_id_type=MESH,
    )

    def spread_tokens(step):
        return pltpu.make_async_remote_copy(
            src_ref=token_got,
            dst_ref=token_all.at[step - 1],
            send_sem=spread_send.at[step - 1],
            recv_sem=spread_recv.at[step - 1],
            device_id={"dp": other_replica(step)},
            device_id_type=MESH,
        )

    def hand_total(step):
        return pltpu.make_async_remote_copy(
            src_ref=token_total,
            dst_ref=token_total,
            send_sem=total_send.at[step - 1],
            recv_sem=total_recv,
            device_id={"tensor": lax.rem(lane + step, tensors)},
            device_id_type=MESH,
        )

    send_segment = pltpu.make_async_remote_copy(
        src_ref=bwd_seg_hbm,
        dst_ref=bwd_seg,
        send_sem=seg_send,
        recv_sem=seg_recv,
        device_id={"pipe": mirror},
        device_id_type=MESH,
    )

    def forward(h):
        load_fwd(h).wait()
        cols = head_span(h)
        probs = softmax(fwd[0, :, cols], fwd[1, :, cols], fwd_bias[...])
        mixed = dot(probs.astype(jnp.bfloat16), fwd[2, :, cols], ((1,), (0,)))
        out[:, cols] = mixed.astype(jnp.bfloat16)

    def first_rows(half):
        part = slice(half * (length // 2), (half + 1) * (length // 2))
        probs = softmax(fwd[0, part, :HEAD_DIM], fwd[1, :, :HEAD_DIM], fwd_bias[part, :])
        mixed = dot(probs.astype(jnp.bfloat16), fwd[2, :, :HEAD_DIM], ((1,), (0,)))
        out[part, :HEAD_DIM] = mixed.astype(jnp.bfloat16)

    seg_copy.wait()
    fwd_bias[...] = mask_bias(fwd_seg[...])
    load_fwd(0).wait()
    first_rows(0)

    @pl.when(relays)
    def _():
        pl.semaphore_wait(barrier, greeted + replicas - 1)

    @pl.when(lane != tensors - 1)
    def _():
        pl.semaphore_wait(barrier, greeted)

    send_first(0).start()
    first_rows(1)
    send_first(1).start()
    send_segment.start()
    tok_copy.wait()
    token_tile[...] = jnp.full(token_tile.shape, tokens[0], jnp.int32)

    @pl.when(relays)
    def _():
        send_tokens.start()

    def exchange(g):
        for step in range(1, tensors):
            send_part(step, g).start()

    for g in range(AHEAD):
        exchange(g)
    pl.loop(2, heads)(lambda h: load_fwd(h).start())
    pl.loop(0, groups)(lambda g: load_own(g).start())
    pl.loop(0, groups)(lambda g: load_up(g).start())

    @pl.loop(1, heads)
    def _(h):
        forward(h)
        send_out(h).start()

        @pl.when(relays & (h == SPREAD_AT))
        def _():
            send_tokens.wait()
            for step in range(1, replicas):
                spread_tokens(step).start()

        @pl.when(relays & (h == TOTAL_AT))
        def _():
            total = token_got[...]
            for step in range(1, replicas):
                spread_tokens(step).wait()
                total += token_all[step - 1]
            token_total[...] = total
            for step in range(1, tensors):
                hand_total(step).start()

    send_segment.wait()
    bwd_bias[...] = mask_bias(bwd_seg[...])

    @pl.when(lane != tensors - 1)
    def _():
        hand_total(1).wait_recv()

    factor = jnp.float32(replicas * length) / token_total[0:1, :].astype(jnp.float32)

    @pl.loop(0, groups)
    def _(g):
        load_own(g).wait()
        load_up(g).wait()
        for step in range(1, tensors):
            recv_part(step, g).wait_recv()

        @pl.when(g < groups - AHEAD)
        def _():
            exchange(g + AHEAD)

        for h in range(GROUP):
            cols = pl.ds(pl.multiple_of(g * width + h * HEAD_DIM, HEAD_DIM), HEAD_DIM)
            query, key, value, upstream = stash[0, :, cols], stash[1, :, cols], stash[2, :, cols], up[:, cols]
            probs = softmax(query, key, bwd_bias[...])
            grad_value = dot(probs.astype(jnp.bfloat16), upstream, ((0,), (0,)))
            grad_probs = dot(upstream, value, ((1,), (1,)))
            center = jnp.sum(probs * grad_probs, axis=-1, keepdims=True)
            grad_logits = (probs * (grad_probs - center) * SCALE).astype(jnp.bfloat16)
            grad_query = dot(grad_logits, key, ((1,), (0,)))
            grad_key = dot(grad_logits, query, ((0,), (0,)))
            grads[0, :, cols] = (grad_query * factor).astype(jnp.bfloat16)
            grads[1, :, cols] = (grad_key * factor).astype(jnp.bfloat16)
            grads[2, :, cols] = (grad_value * factor).astype(jnp.bfloat16)
        send_grads(g).start()

    @pl.when(relays)
    def _():
        for step in range(1, tensors):
            hand_total(step).wait_send()

    @pl.loop(0, groups)
    def _(g):
        for step in range(1, tensors):
            send_part(step, g).wait_send()

    for half in range(2):
        send_first(half).wait()
    pl.loop(1, heads)(lambda h: send_out(h).wait())

    @pl.loop(0, groups)
    def _(g):
        send_grads(g).wait()


def store(received, grads, received_out, grads_out, sems):
    copies = [pltpu.make_async_copy(received, received_out, sems.at[0])]
    for k in range(3):
        copies.append(pltpu.make_async_copy(grads.at[k], grads_out.at[k], sems.at[1 + k]))
    for copy in copies:
        copy.start()
    for copy in copies:
        copy.wait()


def on_device(fwd_qkv, fwd_segments, parked, bwd_segments, grad_out, loss_tokens):
    sections = lax.axis_size("pipe")
    tensors = lax.axis_size("tensor")
    replicas = lax.axis_size("dp")
    length, columns = fwd_qkv.shape[2], fwd_qkv.shape[3]
    heads = columns // HEAD_DIM
    groups = heads // GROUP
    if sections > 2:
        grad_out = lax.ppermute(grad_out, "pipe", [(i, (-i) % sections) for i in range(sections)])
    dma = pltpu.SemaphoreType.DMA
    received, grads = pl.pallas_call(
        functools.partial(kernel, sections, tensors, replicas),
        out_shape=(
            jax.ShapeDtypeStruct((1, length, columns), jnp.bfloat16),
            jax.ShapeDtypeStruct((3, 1, length, columns), jnp.bfloat16),
        ),
        in_specs=[pl.BlockSpec(memory_space=pltpu.HBM)] * 6,
        out_specs=(pl.BlockSpec(memory_space=pl.ANY), pl.BlockSpec(memory_space=pl.ANY)),
        scratch_shapes=[
            pltpu.VMEM((3, length, columns), jnp.bfloat16),
            pltpu.VMEM((length, columns), jnp.bfloat16),
            pltpu.VMEM((3, length, columns), jnp.bfloat16),
            pltpu.VMEM((length, columns), jnp.bfloat16),
            pltpu.VMEM((3, length, columns), jnp.bfloat16),
            pltpu.VMEM((length, length), jnp.float32),
            pltpu.VMEM((length, length), jnp.float32),
            pltpu.VMEM((1, length), jnp.int32),
            pltpu.VMEM((1, length), jnp.int32),
            pltpu.SMEM((1,), jnp.int32),
            pltpu.VMEM((8, HEAD_DIM), jnp.int32),
            pltpu.VMEM((8, HEAD_DIM), jnp.int32),
            pltpu.VMEM((replicas - 1, 8, HEAD_DIM), jnp.int32),
            pltpu.VMEM((8, HEAD_DIM), jnp.int32),
            dma((heads,)), dma((groups,)), dma((groups,)), dma((2,)),
            dma((tensors - 1, groups)), dma((tensors - 1, groups)),
            dma((heads + 1,)), dma((heads + 1,)), dma((groups,)), dma((groups,)),
            dma, dma, dma, dma, dma((replicas - 1,)), dma((replicas - 1,)), dma((tensors - 1,)), dma,
        ],
        compiler_params=pltpu.CompilerParams(
            collective_id=0, has_side_effects=True, vmem_limit_bytes=48 * 1024 * 1024
        ),
        cost_estimate=pl.CostEstimate(
            flops=14 * length * length * columns, bytes_accessed=22 * length * columns, transcendentals=0
        ),
    )(*(pltpu.with_memory_space_constraint(x, pltpu.HBM) for x in (fwd_qkv, fwd_segments, parked, bwd_segments, grad_out)), loss_tokens)
    return pl.pallas_call(
        store,
        out_shape=(
            jax.ShapeDtypeStruct(received.shape, jnp.bfloat16),
            jax.ShapeDtypeStruct(grads.shape, jnp.bfloat16),
        ),
        in_specs=[pl.BlockSpec(memory_space=pl.ANY)] * 2,
        out_specs=(pl.BlockSpec(memory_space=pl.ANY), pl.BlockSpec(memory_space=pl.ANY)),
        scratch_shapes=[dma((4,))],
        compiler_params=pltpu.CompilerParams(vmem_limit_bytes=1024 * 1024),
    )(received, grads)


def solution(mesh):
    placed = (
        P(None, ("pipe", "dp"), None, "tensor"),
        P(("pipe", "dp"), None),
        P(None, ("pipe", "dp"), "tensor", None),
        P(("pipe", "dp"), None),
        P(("pipe", "dp"), None, "tensor"),
        P(("pipe", "dp")),
    )
    return jax.shard_map(
        on_device,
        mesh=mesh,
        in_specs=placed,
        out_specs=(P(("pipe", "dp"), None, "tensor"), P(None, ("pipe", "dp"), None, "tensor")),
        check_vma=False,
    )
```

```python
import functools

import jax
import jax.numpy as jnp
from jax import lax
from jax.experimental import pallas as pl
from jax.experimental.pallas import tpu as pltpu
from jax.sharding import PartitionSpec as P

HEAD_DIM = 128
SCALE = HEAD_DIM ** (-0.5)
GROUP = 2
AHEAD = 2
SPREAD_AT, TOTAL_AT = 2, 6
MESH = pl.DeviceIdType.MESH


def dot(a, b, contract):
    return lax.dot_general(a, b, (contract, ((), ())), preferred_element_type=jnp.float32)


def softmax(query, key, bias):
    logits = dot(query, key, ((1,), (1,))) * SCALE + bias
    weights = jnp.exp(logits - jnp.max(logits, axis=-1, keepdims=True))
    return weights / jnp.sum(weights, axis=-1, keepdims=True)


def mask_bias(segment):
    length = segment.shape[1]
    along = jnp.broadcast_to(segment.astype(jnp.float32), (length, length))
    return jnp.where(along == along.T, jnp.float32(0), jnp.float32(-1e30))


def kernel(
    sections, tensors, replicas,
    fwd_hbm, fwd_seg_hbm, parked_hbm, bwd_seg_hbm, up_hbm, tokens_hbm,
    received_hbm, grads_hbm,
    fwd, out, stash, up, grads, fwd_bias, bwd_bias, fwd_seg, bwd_seg, tokens,
    token_tile, token_got, token_all, token_total,
    fwd_sem, up_sem, own_sem, small_sem,
    part_send, part_recv, out_send, out_recv, grad_send, grad_recv,
    seg_send, seg_recv, tok_send, tok_recv, spread_send, spread_recv, total_send, total_recv,
):
    section = lax.axis_index("pipe")
    lane = lax.axis_index("tensor")
    replica = lax.axis_index("dp")
    after = lax.rem(section + 1, sections)
    before = lax.rem(section + sections - 1, sections)
    mirror = sections - 1 - section
    length = fwd.shape[1]
    width = GROUP * HEAD_DIM
    columns = fwd.shape[2]
    groups = columns // width
    rows = parked_hbm.shape[2]
    heads = columns // HEAD_DIM

    def head_span(h):
        return pl.ds(pl.multiple_of(h * HEAD_DIM, HEAD_DIM), HEAD_DIM)

    def load_fwd(h):
        cols = head_span(h)
        return pltpu.make_async_copy(fwd_hbm.at[:, 0, :, cols], fwd.at[:, :, cols], fwd_sem.at[h])

    seg_copy = pltpu.make_async_copy(fwd_seg_hbm, fwd_seg, small_sem.at[0])
    tok_copy = pltpu.make_async_copy(tokens_hbm, tokens, small_sem.at[1])
    seg_copy.start()
    load_fwd(0).start()

    barrier = pltpu.get_barrier_semaphore()
    greeted = 0
    for step in range(1, tensors):
        pl.semaphore_signal(barrier, inc=1, device_id={"tensor": lax.rem(lane + step, tensors)}, device_id_type=MESH)
        greeted += 1
    pl.semaphore_signal(barrier, inc=1, device_id={"pipe": mirror}, device_id_type=MESH)
    greeted += 1
    if sections > 2:
        for other in (after, before):
            pl.semaphore_signal(barrier, inc=1, device_id={"pipe": other}, device_id_type=MESH)
            greeted += 1

    relays = lane == tensors - 1

    def other_replica(step):
        return lax.rem(replica + step, replicas)

    @pl.when(relays)
    def _():
        for step in range(1, replicas):
            pl.semaphore_signal(barrier, inc=1, device_id={"dp": other_replica(step)}, device_id_type=MESH)

    def span(g):
        return pl.ds(pl.multiple_of(g * width, width), width)

    def load_up(g):
        return pltpu.make_async_copy(up_hbm.at[0, :, span(g)], up.at[:, span(g)], up_sem.at[g])

    def my_rows(who):
        return pl.ds(pl.multiple_of(who * rows, rows), rows)

    def parked_span(who, g):
        return pl.ds(pl.multiple_of(who * columns + g * width, width), width)

    def load_own(g):
        return pltpu.make_async_copy(
            parked_hbm.at[:, 0, :, parked_span(lane, g)], stash.at[:, my_rows(lane), span(g)], own_sem.at[g]
        )

    def send_part(step, g):
        other = lax.rem(lane + step, tensors)
        return pltpu.make_async_remote_copy(
            src_ref=parked_hbm.at[:, 0, :, parked_span(other, g)],
            dst_ref=stash.at[:, my_rows(lane), span(g)],
            send_sem=part_send.at[step - 1, g],
            recv_sem=part_recv.at[step - 1, g],
            device_id={"tensor": other},
            device_id_type=MESH,
        )

    def recv_part(step, g):
        other = lax.rem(lane + tensors - step, tensors)
        return pltpu.make_async_remote_copy(
            src_ref=parked_hbm.at[:, 0, :, parked_span(lane, g)],
            dst_ref=stash.at[:, my_rows(other), span(g)],
            send_sem=part_send.at[step - 1, g],
            recv_sem=part_recv.at[step - 1, g],
            device_id={"tensor": other},
            device_id_type=MESH,
        )

    def send_out(h):
        return pltpu.make_async_remote_copy(
            src_ref=out.at[:, head_span(h)],
            dst_ref=received_hbm.at[0, :, head_span(h)],
            send_sem=out_send.at[h],
            recv_sem=out_recv.at[h],
            device_id={"pipe": after},
            device_id_type=MESH,
        )

    def send_grads(g):
        return pltpu.make_async_remote_copy(
            src_ref=grads.at[:, :, span(g)],
            dst_ref=grads_hbm.at[:, 0, :, span(g)],
            send_sem=grad_send.at[g],
            recv_sem=grad_recv.at[g],
            device_id={"pipe": mirror},
            device_id_type=MESH,
        )

    send_tokens = pltpu.make_async_remote_copy(
        src_ref=token_tile,
        dst_ref=token_got,
        send_sem=tok_send,
        recv_sem=tok_recv,
        device_id={"pipe": mirror},
        device_id_type=MESH,
    )

    def spread_tokens(step):
        return pltpu.make_async_remote_copy(
            src_ref=token_got,
            dst_ref=token_all.at[step - 1],
            send_sem=spread_send.at[step - 1],
            recv_sem=spread_recv.at[step - 1],
            device_id={"dp": other_replica(step)},
            device_id_type=MESH,
        )

    def hand_total(step):
        return pltpu.make_async_remote_copy(
            src_ref=token_total,
            dst_ref=token_total,
            send_sem=total_send.at[step - 1],
            recv_sem=total_recv,
            device_id={"tensor": lax.rem(lane + step, tensors)},
            device_id_type=MESH,
        )

    send_segment = pltpu.make_async_remote_copy(
        src_ref=bwd_seg_hbm,
        dst_ref=bwd_seg,
        send_sem=seg_send,
        recv_sem=seg_recv,
        device_id={"pipe": mirror},
        device_id_type=MESH,
    )

    def forward(h):
        load_fwd(h).wait()
        cols = head_span(h)
        probs = softmax(fwd[0, :, cols], fwd[1, :, cols], fwd_bias[...])
        mixed = dot(probs.astype(jnp.bfloat16), fwd[2, :, cols], ((1,), (0,)))
        out[:, cols] = mixed.astype(jnp.bfloat16)

    tok_copy.start()
    pl.loop(1, heads)(lambda h: load_fwd(h).start())
    seg_copy.wait()
    fwd_bias[...] = mask_bias(fwd_seg[...])
    forward(0)
    tok_copy.wait()
    token_tile[...] = jnp.full(token_tile.shape, tokens[0], jnp.int32)

    @pl.when(relays)
    def _():
        pl.semaphore_wait(barrier, greeted + replicas - 1)
        send_tokens.start()

    @pl.when(lane != tensors - 1)
    def _():
        pl.semaphore_wait(barrier, greeted)

    send_segment.start()
    send_out(0).start()

    def exchange(g):
        for step in range(1, tensors):
            send_part(step, g).start()

    for g in range(AHEAD):
        exchange(g)
    pl.loop(0, groups)(lambda g: load_own(g).start())
    pl.loop(0, groups)(lambda g: load_up(g).start())

    @pl.loop(1, heads)
    def _(h):
        forward(h)
        send_out(h).start()

        @pl.when(relays & (h == SPREAD_AT))
        def _():
            send_tokens.wait()
            for step in range(1, replicas):
                spread_tokens(step).start()

        @pl.when(relays & (h == TOTAL_AT))
        def _():
            total = token_got[...]
            for step in range(1, replicas):
                spread_tokens(step).wait()
                total += token_all[step - 1]
            token_total[...] = total
            for step in range(1, tensors):
                hand_total(step).start()

    send_segment.wait()
    bwd_bias[...] = mask_bias(bwd_seg[...])

    @pl.when(lane != tensors - 1)
    def _():
        hand_total(1).wait_recv()

    factor = jnp.float32(replicas * length) / token_total[0:1, :].astype(jnp.float32)

    @pl.loop(0, groups)
    def _(g):
        load_own(g).wait()
        load_up(g).wait()
        for step in range(1, tensors):
            recv_part(step, g).wait_recv()

        @pl.when(g < groups - AHEAD)
        def _():
            exchange(g + AHEAD)

        spans = [pl.ds(pl.multiple_of(g * width + h * HEAD_DIM, HEAD_DIM), HEAD_DIM) for h in range(GROUP)]
        logits = [dot(stash[1, :, cols], stash[0, :, cols], ((1,), (1,))) * SCALE + bwd_bias[...] for cols in spans]
        grad_probs = [dot(stash[2, :, cols], up[:, cols], ((1,), (1,))) for cols in spans]
        probs = []
        for tile in logits:
            weights = jnp.exp(tile - jnp.max(tile, axis=0, keepdims=True))
            probs.append(weights * (1.0 / jnp.sum(weights, axis=0, keepdims=True)))
        for cols, tile in zip(spans, probs):
            grad_value = dot(tile.astype(jnp.bfloat16), up[:, cols], ((1,), (0,)))
            grads[2, :, cols] = (grad_value * factor).astype(jnp.bfloat16)
        grad_logits = []
        for tile, grad in zip(probs, grad_probs):
            center = jnp.sum(tile * grad, axis=0, keepdims=True)
            grad_logits.append((tile * (grad - center) * SCALE).astype(jnp.bfloat16))
        for cols, tile in zip(spans, grad_logits):
            grad_key = dot(tile, stash[0, :, cols], ((1,), (0,)))
            grads[1, :, cols] = (grad_key * factor).astype(jnp.bfloat16)
            grad_query = dot(tile, stash[1, :, cols], ((0,), (0,)))
            grads[0, :, cols] = (grad_query * factor).astype(jnp.bfloat16)
        send_grads(g).start()

    @pl.when(relays)
    def _():
        for step in range(1, tensors):
            hand_total(step).wait_send()

    @pl.loop(0, groups)
    def _(g):
        for step in range(1, tensors):
            send_part(step, g).wait_send()

    pl.loop(0, heads)(lambda h: send_out(h).wait())

    @pl.loop(0, groups)
    def _(g):
        send_grads(g).wait()


def store(received, grads, received_out, grads_out, sems):
    copies = [pltpu.make_async_copy(received, received_out, sems.at[0])]
    for k in range(3):
        copies.append(pltpu.make_async_copy(grads.at[k], grads_out.at[k], sems.at[1 + k]))
    for copy in copies:
        copy.start()
    for copy in copies:
        copy.wait()


def on_device(fwd_qkv, fwd_segments, parked, bwd_segments, grad_out, loss_tokens):
    sections = lax.axis_size("pipe")
    tensors = lax.axis_size("tensor")
    replicas = lax.axis_size("dp")
    length, columns = fwd_qkv.shape[2], fwd_qkv.shape[3]
    heads = columns // HEAD_DIM
    groups = heads // GROUP
    if sections > 2:
        grad_out = lax.ppermute(grad_out, "pipe", [(i, (-i) % sections) for i in range(sections)])
    dma = pltpu.SemaphoreType.DMA
    received, grads = pl.pallas_call(
        functools.partial(kernel, sections, tensors, replicas),
        out_shape=(
            jax.ShapeDtypeStruct((1, length, columns), jnp.bfloat16),
            jax.ShapeDtypeStruct((3, 1, length, columns), jnp.bfloat16),
        ),
        in_specs=[pl.BlockSpec(memory_space=pltpu.HBM)] * 6,
        out_specs=(pl.BlockSpec(memory_space=pl.ANY), pl.BlockSpec(memory_space=pl.ANY)),
        scratch_shapes=[
            pltpu.VMEM((3, length, columns), jnp.bfloat16),
            pltpu.VMEM((length, columns), jnp.bfloat16),
            pltpu.VMEM((3, length, columns), jnp.bfloat16),
            pltpu.VMEM((length, columns), jnp.bfloat16),
            pltpu.VMEM((3, length, columns), jnp.bfloat16),
            pltpu.VMEM((length, length), jnp.float32),
            pltpu.VMEM((length, length), jnp.float32),
            pltpu.VMEM((1, length), jnp.int32),
            pltpu.VMEM((1, length), jnp.int32),
            pltpu.SMEM((1,), jnp.int32),
            pltpu.VMEM((8, HEAD_DIM), jnp.int32),
            pltpu.VMEM((8, HEAD_DIM), jnp.int32),
            pltpu.VMEM((replicas - 1, 8, HEAD_DIM), jnp.int32),
            pltpu.VMEM((8, HEAD_DIM), jnp.int32),
            dma((heads,)), dma((groups,)), dma((groups,)), dma((2,)),
            dma((tensors - 1, groups)), dma((tensors - 1, groups)),
            dma((heads,)), dma((heads,)), dma((groups,)), dma((groups,)),
            dma, dma, dma, dma, dma((replicas - 1,)), dma((replicas - 1,)), dma((tensors - 1,)), dma,
        ],
        compiler_params=pltpu.CompilerParams(
            collective_id=0, has_side_effects=True, vmem_limit_bytes=48 * 1024 * 1024
        ),
        cost_estimate=pl.CostEstimate(
            flops=14 * length * length * columns, bytes_accessed=22 * length * columns, transcendentals=0
        ),
    )(*(pltpu.with_memory_space_constraint(x, pltpu.HBM) for x in (fwd_qkv, fwd_segments, parked, bwd_segments, grad_out)), loss_tokens)
    return pl.pallas_call(
        store,
        out_shape=(
            jax.ShapeDtypeStruct(received.shape, jnp.bfloat16),
            jax.ShapeDtypeStruct(grads.shape, jnp.bfloat16),
        ),
        in_specs=[pl.BlockSpec(memory_space=pl.ANY)] * 2,
        out_specs=(pl.BlockSpec(memory_space=pl.ANY), pl.BlockSpec(memory_space=pl.ANY)),
        scratch_shapes=[dma((4,))],
        compiler_params=pltpu.CompilerParams(vmem_limit_bytes=1024 * 1024),
    )(received, grads)


def solution(mesh):
    placed = (
        P(None, ("pipe", "dp"), None, "tensor"),
        P(("pipe", "dp"), None),
        P(None, ("pipe", "dp"), "tensor", None),
        P(("pipe", "dp"), None),
        P(("pipe", "dp"), None, "tensor"),
        P(("pipe", "dp")),
    )
    return jax.shard_map(
        on_device,
        mesh=mesh,
        in_specs=placed,
        out_specs=(P(("pipe", "dp"), None, "tensor"), P(None, ("pipe", "dp"), None, "tensor")),
        check_vma=False,
    )
```
